512 devices in a mesh: gx: 8 (over x, core), gy: 16 (over z), gz: 4 (over y).
Axes of the slice: x: 4, y: 4, z: 16, core: 2. Of those that a mesh axis runs over, the one named last changes fastest.
Arguments:
- positions: float32 [3, 8, 16, 4, 1024], P(None, 'gx', 'gy', 'gz'), may hold values from 0 to 1
- velocities: float32 [3, 8, 16, 4, 1024], P(None, 'gx', 'gy', 'gz'), may hold values from -2.5 to 2.5
- forces: float32 [3, 8, 16, 4, 1024], P(None, 'gx', 'gy', 'gz'), may hold values from -6 to 6
- counts: int32 [8, 16, 4], P('gx', 'gy', 'gz'), may hold values from 512 to 1024, as said below
- pair_tiles: int32 [2, 8, 16, 4, 128], P(None, 'gx', 'gy', 'gz'), may hold values from 0 to 287, as said below
- pair_count: int32 [8, 16, 4], P('gx', 'gy', 'gz'), may hold values from 16 to 128, as said below
- mig_slots: int32 [2, 4, 8, 16, 4, 128], P(None, None, 'gx', 'gy', 'gz'), may hold values from 0 to 511, as said below
Outputs:
- final_positions: float32 [3, 8, 16, 4, 1024], P(None, 'gx', 'gy', 'gz')
- final_velocities: float32 [3, 8, 16, 4, 1024], P(None, 'gx', 'gy', 'gz')
The draws below stay inside these ranges and needn't reach their ends.
Inputs may be any that keep to these rules, and one draw needn't show every extreme that they name: `counts`: a brick's live atoms fill its first slots. `pair_count`: a brick's live list entries are its first ones. `pair_tiles`: row 0 holds a tile below 8, row 1 a ghost tile of the brick's neighbourhood. `mig_slots`: in each step and brick the 512 slots are distinct and below 512.
All inputs are finite; a program needn't handle non-finite values.
Results may differ from the reference program's by a relative error of at most 0.0003.
Values sent between devices are 32-bit elements; how exact they have to be, the bound alone decides.
No kernel may reach another device: no remote copies, remote signals or barrier semaphores. Data moves between devices by JAX's collectives and lax.ppermute only.
A program may use at most 64 MiB of HBM per device.

```python
import jax
import jax.numpy as jnp
from jax import lax

ROWS = 1024
PAIRS = 128
MIG = 128
STEPS = 2
TILES = 8
NBX = 8
NBY = 16
NBZ = 4


def draw_positions(key, part):
    key = jax.random.fold_in(key, 15)
    key_side, key_face, key_height = jax.random.split(key, 3)
    extent = (2, NBX, NBY, NBZ, ROWS)
    inner_low = 0.43
    inner_high = 0.57
    rim_width = 0.07
    fraction = jax.random.uniform(key_side, extent, jnp.float32)
    near_low = jax.random.bernoulli(key_face, 0.5, extent)
    rim_value = jnp.where(near_low, rim_width * fraction, 1.0 - rim_width * fraction)
    inner_value = inner_low + (inner_high - inner_low) * fraction
    odd_lane = jnp.arange(ROWS, dtype=jnp.int32) % 2 == 1
    flat_part = jnp.where(odd_lane, rim_value, inner_value)
    height = jax.random.uniform(key_height, (1, NBX, NBY, NBZ, ROWS), jnp.float32)
    return jnp.concatenate([flat_part, height], axis=0).astype(jnp.float32)


def draw_counts(key, part):
    key = jax.random.fold_in(key, 11)
    key_one, key_two = jax.random.split(key)
    bricks = NBX * NBY * NBZ
    values = jax.random.randint(key_one, (bricks,), ROWS // 2, ROWS + 1)
    chosen = jax.random.randint(key_two, (), 0, bricks)
    values = values.at[chosen].set(ROWS)
    values = values.at[(chosen + 1) % bricks].set(ROWS // 2)
    return values.reshape(NBX, NBY, NBZ).astype(jnp.int32)


def draw_pair_count(key, part):
    key = jax.random.fold_in(key, 12)
    key_one, key_two = jax.random.split(key)
    bricks = NBX * NBY * NBZ
    powers = jax.random.randint(key_one, (bricks,), 0, 4)
    values = PAIRS // 8 * jnp.power(2, powers)
    chosen = jax.random.randint(key_two, (), 0, bricks)
    values = values.at[chosen].set(PAIRS)
    return values.reshape(NBX, NBY, NBZ).astype(jnp.int32)


def draw_pair_tiles(key, part):
    key = jax.random.fold_in(key, 13)
    key_one, key_two = jax.random.split(key)
    extent = (NBX, NBY, NBZ, PAIRS)
    local_tile = jax.random.randint(key_one, extent, 0, TILES)
    ghost_tile = jax.random.randint(key_two, extent, 0, 9 * NBZ * TILES)
    ghost_tile = ghost_tile.at[0, 0, 0, 0].set(9 * NBZ * TILES - 1)
    return jnp.stack([local_tile, ghost_tile]).astype(jnp.int32)


def draw_mig_slots(key, part):
    key = jax.random.fold_in(key, 14)
    bricks = NBX * NBY * NBZ
    key_list = jax.random.split(key, STEPS * bricks)
    chosen = jax.vmap(lambda key_each: jax.random.permutation(key_each, ROWS // 2)[:4 * MIG])(key_list)
    chosen = chosen.reshape(STEPS, NBX, NBY, NBZ, 4, MIG).transpose(0, 4, 1, 2, 3, 5)
    return chosen.astype(jnp.int32)


def shard_levels(own_key, shape, pieces, smallest, top_value):
    def one(axis_at, shards_of):
        steps = jax.random.uniform(jax.random.fold_in(jax.random.fold_in(own_key, 6), axis_at), (shards_of,), jnp.float32, smallest / len(pieces), top_value / len(pieces))
        return jnp.repeat(jnp.exp(steps), shape[axis_at] // shards_of).reshape((-1,) + (1,) * (len(shape) - axis_at - 1))

    factor_of = one(*pieces[0])
    for cut in pieces[1:]:
        factor_of = factor_of * one(*cut)
    return factor_of


def scatter_about(key, dims, scale, bound, pieces=(), kind=jnp.bfloat16):
    values = scale * jax.random.normal(key, dims, jnp.float32)
    if pieces:
        values = values * shard_levels(key, dims, pieces, -0.22, 0.18)
    return jnp.clip(values, -bound, bound).astype(kind)


def setup_inputs(seed: int = 0) -> dict:
    splits = jax.random.split(jax.random.key(seed), 8)
    return {
        "positions": draw_positions(jax.random.fold_in(splits[7], 71), 0),
        "velocities": scatter_about(splits[1], (3, NBX, NBY, NBZ, ROWS), 0.25, 2.5, ((1, 8), (2, 16), (3, 4)), jnp.float32),
        "forces": scatter_about(splits[2], (3, NBX, NBY, NBZ, ROWS), 1.0, 6.0, ((1, 8), (2, 16), (3, 4)), jnp.float32),
        "counts": draw_counts(jax.random.fold_in(splits[7], 71), 0),
        "pair_tiles": draw_pair_tiles(jax.random.fold_in(splits[7], 71), 0),
        "pair_count": draw_pair_count(jax.random.fold_in(splits[7], 71), 0),
        "mig_slots": draw_mig_slots(jax.random.fold_in(splits[7], 71), 0),
    }


box_edge = 1.0
cutoff_sq = 0.81
height_ratio = 0.25
density_scale = 1.0 / 256.0
repulsion = 1.0 / 512.0
embed_scale = 1.0
time_step = 0.25

def geometry(own_rows, ghost_rows, local_tile, ghost_tile, in_list, selfbase):
    near_tiles = jnp.take(own_rows.reshape(4, -1, 128), local_tile, axis=1)
    far_tiles = jnp.take(ghost_rows.reshape(4, -1, 128), ghost_tile, axis=1)
    raw_offset = near_tiles[:3, :, :, None] - far_tiles[:3, :, None, :]
    offset_vec = jnp.stack([raw_offset[0], raw_offset[1], height_ratio * raw_offset[2]])
    dist_sq = offset_vec[0] * offset_vec[0] + offset_vec[1] * offset_vec[1] + offset_vec[2] * offset_vec[2]
    shrink = jnp.maximum(1.0 - dist_sq / cutoff_sq, 0.0)
    lane_ids = jnp.arange(128, dtype=jnp.int32)
    same_atom = (ghost_tile == local_tile + selfbase)[:, None, None] & (lane_ids[:, None] == lane_ids[None, :])[None]
    weight = near_tiles[3][:, :, None] * far_tiles[3][:, None, :] * in_list.astype(jnp.float32)[:, None, None]
    weight = jnp.where(same_atom, 0.0, weight)
    return (offset_vec, shrink, weight)

def tile_sum(row_terms, local_tile, tile_count):
    onehot = (local_tile[:, None] == jnp.arange(tile_count, dtype=jnp.int32)[None, :]).astype(jnp.float32)
    return jnp.einsum('pt,...pr->...tr', onehot, row_terms, precision=lax.Precision.HIGHEST)

def density_rows(shrink, weight):
    return lax.optimization_barrier(jnp.sum(weight * shrink ** 3, axis=2)) * density_scale

def force_rows(offset_vec, shrink, weight, near_fp, far_fp):
    slope_sum = -4.0 * repulsion * shrink ** 3 / cutoff_sq + (near_fp[:, :, None] + far_fp[:, None, :]) * (-3.0 * density_scale * shrink ** 2 / cutoff_sq)
    coefficient = 2.0 * weight * slope_sum
    return -lax.optimization_barrier(jnp.sum(coefficient[None] * offset_vec, axis=3))

def ghost_offsets(zbrick, tower_size):
    side_shift = (jnp.arange(3, dtype=jnp.int32) - 1).astype(jnp.float32) * box_edge
    depth_shift = (jnp.arange(tower_size, dtype=jnp.int32) - zbrick).astype(jnp.float32) * box_edge
    extent = (3, 3, tower_size, 1)
    return jnp.stack([jnp.broadcast_to(side_shift[:, None, None, None], extent), jnp.broadcast_to(side_shift[None, :, None, None], extent), jnp.broadcast_to(depth_shift[None, None, :, None], extent)])

def plate_cells(values_in, brick_x, brick_y):
    rows_x = (brick_x + jnp.arange(3, dtype=jnp.int32) - 1) % NBX
    rows_y = (brick_y + jnp.arange(3, dtype=jnp.int32) - 1) % NBY
    return jnp.take(jnp.take(values_in, rows_x, axis=1), rows_y, axis=2)

def locate(brick_index):
    return (brick_index // (NBY * NBZ), brick_index // NBZ % NBY, brick_index % NBZ)

def advance(positions, velocities):
    return jnp.concatenate([positions[:2] + time_step * velocities[:2], positions[2:] + time_step / height_ratio * velocities[2:]], axis=0)

def evaluate(positions, live, pair_tiles, pair_count):
    with_live = jnp.concatenate([positions, live[None]], axis=0)
    tile_count = ROWS // 128

    def brick_setup(brick_index):
        brick_x, brick_y, brick_z = locate(brick_index)
        cells = plate_cells(with_live, brick_x, brick_y)
        ghost_rows = jnp.concatenate([cells[:3] + ghost_offsets(brick_z, NBZ), cells[3:]], axis=0).reshape(4, -1)
        own_rows = with_live[:, brick_x, brick_y, brick_z]
        local_tile = pair_tiles[0, brick_x, brick_y, brick_z]
        ghost_tile = pair_tiles[1, brick_x, brick_y, brick_z]
        in_list = jnp.arange(PAIRS, dtype=jnp.int32) < pair_count[brick_x, brick_y, brick_z]
        selfbase = (4 * NBZ + brick_z) * tile_count
        return (geometry(own_rows, ghost_rows, local_tile, ghost_tile, in_list, selfbase), local_tile, ghost_tile)

    def density_one(brick_index):
        pair_parts, local_tile, ghost_tile = brick_setup(brick_index)
        return tile_sum(density_rows(pair_parts[1], pair_parts[2]), local_tile, tile_count).reshape(ROWS)
    bricks = NBX * NBY * NBZ
    density = lax.map(density_one, jnp.arange(bricks, dtype=jnp.int32)).reshape(NBX, NBY, NBZ, ROWS)
    slope_fp = -0.5 * embed_scale / jnp.sqrt(1.0 + density)

    def force_one(brick_index):
        pair_parts, local_tile, ghost_tile = brick_setup(brick_index)
        brick_x, brick_y, brick_z = locate(brick_index)
        far_all = plate_cells(slope_fp[None], brick_x, brick_y).reshape(-1, 128)
        near_fp = jnp.take(slope_fp[brick_x, brick_y, brick_z].reshape(tile_count, 128), local_tile, axis=0)
        far_fp = jnp.take(far_all, ghost_tile, axis=0)
        terms = force_rows(pair_parts[0], pair_parts[1], pair_parts[2], near_fp, far_fp)
        return tile_sum(terms, local_tile, tile_count).reshape(3, ROWS)
    pushes = lax.map(force_one, jnp.arange(bricks, dtype=jnp.int32))
    return pushes.reshape(NBX, NBY, NBZ, 3, ROWS).transpose(3, 0, 1, 2, 4)

def place_rows(state_rows, where, arrived):
    return state_rows.at[:, where].set(arrived)

def migrate(positions, velocities, slots):
    state_rows = jnp.concatenate([positions, velocities], axis=0)
    bricks = NBX * NBY * NBZ
    result = state_rows.reshape(6, bricks, ROWS)
    plan_list = ((-1, 1, 1, 0, 1.0), (1, 1, 0, 0, -1.0), (-1, 2, 3, 1, 1.0), (1, 2, 2, 1, -1.0))
    for direction, (roll_by, axis_num, their_list, component, direction_sign) in enumerate(plan_list):
        source = jnp.roll(state_rows, roll_by, axis=axis_num)
        their_slots = jnp.roll(slots[their_list], roll_by, axis=axis_num - 1)
        their_slots = jnp.broadcast_to(their_slots[None], (6,) + their_slots.shape)
        arrived = jnp.take_along_axis(source, their_slots, axis=4)
        arrived = arrived.at[component].add(direction_sign * box_edge)
        result = jax.vmap(place_rows, in_axes=(1, 0, 1), out_axes=1)(result, slots[direction].reshape(bricks, MIG), arrived.reshape(6, bricks, MIG))
    result = result.reshape(6, NBX, NBY, NBZ, ROWS)
    return (result[:3], result[3:])

def reference(positions, velocities, forces, counts, pair_tiles, pair_count, mig_slots):
    live = (jnp.arange(ROWS, dtype=jnp.int32)[None, None, None, :] < counts[:, :, :, None]).astype(jnp.float32)
    for step_index in range(STEPS):
        velocities = velocities + 0.5 * time_step * forces
        positions = advance(positions, velocities)
        positions, velocities = migrate(positions, velocities, mig_slots[step_index])
        forces = evaluate(positions, live, pair_tiles, pair_count)
        velocities = velocities + 0.5 * time_step * forces
    return (positions, velocities)
```

```python
import functools

import jax
import jax.numpy as jnp
from jax import lax
from jax.experimental import pallas as pl
from jax.experimental.pallas import tpu as pltpu
from jax.sharding import PartitionSpec as P

cutoff_sq = 0.81
cutoff = 0.9
height_ratio = 0.25
density_scale = 1.0 / 256.0
repulsion = 1.0 / 512.0
time_step = 0.25
kick = 0.5 * time_step
flat_scale = 1.0 / cutoff
tall_scale = height_ratio / cutoff
cube_factor = -8.0 * repulsion / cutoff_sq
slope_factor = -6.0 * density_scale / cutoff_sq
far_away = 1e15

VMEM = pl.BlockSpec(memory_space=pltpu.VMEM)
ANY = pl.BlockSpec(memory_space=pl.ANY)
SMEM = pl.BlockSpec(memory_space=pltpu.SMEM)
params = pltpu.CompilerParams(vmem_limit_bytes=24 * 1024 * 1024)
unrolled = 4
nt_dims = (((1,), (1,)), ((), ()))
nn_dims = (((1,), (0,)), ((), ()))


def dot(left, right, dims):
    return lax.dot_general(left, right, dims, preferred_element_type=jnp.float32)


def pieces(values, count):
    out = []
    for _ in range(count):
        part = values.astype(jnp.bfloat16)
        out.append(part)
        values = values - part.astype(jnp.float32)
    return out


def slot_masks(slots_ref, direction):
    slots = slots_ref[direction : direction + 1, :]
    lane_hit = lax.broadcasted_iota(jnp.int32, (128, 128), 0) == (slots & 127)
    tile_hit = lax.broadcasted_iota(jnp.int32, (8, 128), 0) == (slots >> 7)
    return jnp.where(lane_hit, 1.0, 0.0).astype(jnp.bfloat16), tile_hit


def drift_and_pack(place, speed, push, slots_ref, place_ref, speed_ref, packed_refs):
    speed = [speed[c] + kick * push[c] for c in range(3)]
    rates = (time_step, time_step, time_step / height_ratio)
    place = [place[c] + rates[c] * speed[c] for c in range(3)]
    for c in range(3):
        place_ref[c] = place[c]
        speed_ref[c] = speed[c]
    rows = jnp.concatenate(place + speed, axis=0)
    split = jnp.concatenate(pieces(rows, 3), axis=0)
    for direction in range(4):
        lane_hit, tile_hit = slot_masks(slots_ref, direction)
        found = dot(split, lane_hit, nn_dims)
        found = found[0:48] + found[48:96] + found[96:144]
        for c in range(6):
            chosen = jnp.where(tile_hit, found[8 * c : 8 * c + 8], 0.0)
            packed_refs[direction][c : c + 1, :] = jnp.sum(chosen, axis=0, keepdims=True)
        packed_refs[direction][6:8, :] = jnp.zeros((2, 128), jnp.float32)


def pack_kernel(
    place_in,
    speed_in,
    push_in,
    slots_in,
    place_ref,
    speed_ref,
    p0,
    p1,
    p2,
    p3,
    slots_out,
    place_at,
    speed_at,
    push_at,
    sems,
):
    pairs = (
        (place_in, place_at),
        (speed_in, speed_at),
        (push_in, push_at),
        (slots_in, slots_out),
    )
    copies = [
        pltpu.make_async_copy(here, there, sems.at[i]) for i, (here, there) in enumerate(pairs)
    ]
    for copy in copies:
        copy.start()
    for copy in copies:
        copy.wait()
    drift_and_pack(
        [place_at[c] for c in range(3)],
        [speed_at[c] for c in range(3)],
        [push_at[c] for c in range(3)],
        slots_out.at[0],
        place_ref,
        speed_ref,
        (p0, p1, p2, p3),
    )


def unpack_kernel(
    step, count_ref, place_in, speed_in, slots_in, a0, a1, a2, a3, place_ref, speed_ref, sent_ref
):
    slots_ref = slots_in.at[step]
    total = jnp.zeros((160, 128), jnp.float32)
    plan = ((a0, 0, 1.0), (a1, 0, -1.0), (a2, 1, 1.0), (a3, 1, -1.0))
    for direction, (arrived, component, shift) in enumerate(plan):
        lane_hit, tile_hit = slot_masks(slots_ref, direction)
        rows = []
        for c in range(6):
            row = arrived[c : c + 1, :]
            if c == component:
                row = row + shift
            rows.append(jnp.where(tile_hit, row, 0.0))
        marks = jnp.where(tile_hit, 1.0, 0.0)
        split = pieces(jnp.concatenate(rows, axis=0), 3)
        split.append(jnp.concatenate([marks, jnp.zeros_like(marks)], axis=0).astype(jnp.bfloat16))
        total = total + dot(jnp.concatenate(split, axis=0), lane_hit, nt_dims)
    put = total[0:48] + total[48:96] + total[96:144]
    taken = total[144:152] > 0.5
    slot_ids = lax.broadcasted_iota(jnp.int32, (8, 128), 0) * 128 + lax.broadcasted_iota(
        jnp.int32, (8, 128), 1
    )
    live = slot_ids < count_ref[0]
    scales = (flat_scale, flat_scale, tall_scale)
    for c in range(3):
        place = jnp.where(taken, put[8 * c : 8 * c + 8], place_in[c])
        place_ref[c] = place
        speed_ref[c] = jnp.where(taken, put[24 + 8 * c : 32 + 8 * c], speed_in[c])
        sent_ref[c] = jnp.where(live, place * scales[c], far_away)


def put_ghosts(cells, ghost_ref):
    zbrick = lax.axis_index("gz")
    for level in range(4):
        rise = ((level - zbrick).astype(jnp.float32) - 0.5) * tall_scale
        for dx, cell in enumerate(cells):
            for dy in range(3):
                brick = dx * 12 + dy * 4 + level
                ghost_ref[brick, 0] = cell[level, dy, 0] + (dx - 1.5) * flat_scale
                ghost_ref[brick, 1] = cell[level, dy, 1] + (dy - 1.5) * flat_scale
                ghost_ref[brick, 2] = cell[level, dy, 2] + rise
    ghost_ref[36] = jnp.full(ghost_ref.shape[1:], far_away, jnp.float32)


def own_places(middle):
    zbrick = lax.axis_index("gz")
    own = [middle[zbrick, 1, c] for c in range(3)]
    live = own[0] < 0.5 * far_away
    shifts = (0.5 * flat_scale, 0.5 * flat_scale, 0.5 * tall_scale)
    return [jnp.where(live, row - shift, -far_away) for row, shift in zip(own, shifts)], live


def eight(row):
    return jnp.broadcast_to(row, (8, 128))


def in_three(values):
    first = values.astype(jnp.bfloat16).astype(jnp.float32)
    values = values - first
    second = values.astype(jnp.bfloat16).astype(jnp.float32)
    third = (values - second).astype(jnp.bfloat16).astype(jnp.float32)
    return first, second, third


def sublanes():
    return lax.broadcasted_iota(jnp.int32, (8, 128), 0)


def by_rows(at, rows):
    out = jnp.zeros((8, 128), jnp.float32)
    for i, row in enumerate(rows):
        if row is not None:
            out = jnp.where(at == i, row, out)
    return out


def near_factors(places, slopes):
    at = sublanes()
    x, y, z = (eight(row) for row in places)
    rest = 0.5 - (x * x + y * y + z * z)
    at_flat = jnp.where(at >= 4, at - 4, at)
    mixed = jnp.where(at_flat == 0, x, jnp.where(at_flat == 1, y, z))
    first, second, third = in_three(mixed)
    ends = in_three(rest)
    blocks = []
    for later, end in zip((second, second, third), ends):
        block = 2.0 * jnp.where(at < 4, first, later)
        block = jnp.where(at == 3, 1.0, jnp.where(at == 7, end, block))
        blocks.append(block)
    none = jnp.zeros((8, 128), jnp.float32)
    plain = jnp.concatenate(blocks + [none], axis=0).T
    if slopes is None:
        return plain.astype(jnp.bfloat16)
    one, two, three = in_three(eight(slopes))
    sloped = by_rows(at, (one, two, three, 1.0, 1.0, 1.0))
    sloped = jnp.concatenate(blocks + [sloped], axis=0).T
    return jnp.concatenate([plain, sloped], axis=0).astype(jnp.bfloat16)


def far_factors(places, slopes):
    at = sublanes()
    x, y, z = (eight(row) for row in places)
    rest = 0.5 - (x * x + y * y + z * z)
    at_flat = jnp.where(at >= 4, at - 4, at)
    mixed = jnp.where(at_flat == 0, x, jnp.where(at_flat == 1, y, jnp.where(at == 3, rest, z)))
    first, second, third = in_three(mixed)
    last = at == 7
    blocks = [
        jnp.where(last, 1.0, first),
        jnp.where(last, 1.0, second),
        jnp.where(last, 1.0, jnp.where(at < 4, third, first)),
    ]
    if slopes is None:
        blocks.append(jnp.zeros((8, 128), jnp.float32))
    else:
        one, two, three = in_three(eight(slopes))
        blocks.append(by_rows(at, (1.0, 1.0, 1.0, one, two, three)))
    summed = jnp.where(at == 3, 1.0, jnp.where(at < 4, first, second))
    summed = jnp.concatenate([summed, third], axis=0).astype(jnp.bfloat16)
    return jnp.concatenate(blocks, axis=0).astype(jnp.bfloat16), summed


def entry(tiles_ref, number, total):
    listed = number < total
    near = jnp.where(listed, tiles_ref[0, number], 0)
    far = tiles_ref[1, number]
    return near, far, jnp.where(listed, far >> 3, 36), far & 7, listed


def halves(block):
    first = block.astype(jnp.bfloat16)
    second = (block - first.astype(jnp.float32)).astype(jnp.bfloat16)
    return jnp.concatenate([first, second], axis=1)


def density_kernel(
    total_ref,
    tiles_in,
    behind,
    middle,
    ahead,
    slope_ref,
    tiles_ref,
    ghost_ref,
    near_ref,
    sum_ref,
    row_ref,
    sem,
):
    copy = pltpu.make_async_copy(tiles_in, tiles_ref, sem)
    copy.start()
    zbrick = lax.axis_index("gz")
    put_ghosts((behind, middle, ahead), ghost_ref)
    own, live = own_places(middle)
    for t in range(8):
        near_ref[t] = near_factors([row[t : t + 1] for row in own], None)
    sum_ref[...] = jnp.zeros_like(sum_ref)
    tile_ids = sublanes()
    total = total_ref[0]
    copy.wait()

    def add(group, selves):
        for part in range(unrolled):
            near, far, brick, tile, listed = entry(tiles_ref, group * unrolled + part, total)
            places = [ghost_ref[brick, c, pl.ds(tile, 1), :] for c in range(3)]
            factors, _ = far_factors(places, None)
            shrink = jnp.maximum(dot(near_ref[near], factors, nn_dims), 0.0)
            sum_ref[near] += shrink * shrink * shrink
            same = jnp.logical_and(listed, far == (16 + zbrick) * 8 + near)
            selves = selves + jnp.where(tile_ids == jnp.where(same, near, -1), 1.0, 0.0)
        return selves

    selves = lax.fori_loop(
        0, (total + unrolled - 1) // unrolled, add, jnp.zeros((8, 128), jnp.float32)
    )
    ones = jnp.ones((16, 256), jnp.bfloat16)
    for t in range(8):
        row_ref[t : t + 1, :] = dot(ones, halves(sum_ref[t]), nt_dims)[0:1]
    density = (row_ref[...] - jnp.where(live, selves, 0.0)) * density_scale
    slope_ref[...] = (-0.5 * slope_factor / cube_factor) / jnp.sqrt(1.0 + density)


def force_sums(
    total_ref,
    tiles_in,
    cells,
    slope_cells,
    own_slope,
    tiles_ref,
    ghost_ref,
    near_ref,
    sum_ref,
    push_ref,
    sem,
):
    copy = pltpu.make_async_copy(tiles_in, tiles_ref, sem)
    copy.start()
    put_ghosts(cells, ghost_ref)
    for dy, cell in enumerate(slope_cells):
        for dx in range(3):
            for level in range(4):
                ghost_ref[dx * 12 + dy * 4 + level, 3] = cell[dx * 4 + level]
    own, _ = own_places(cells[1])
    for t in range(8):
        near_ref[t] = near_factors([row[t : t + 1] for row in own], own_slope[t : t + 1, :])
    sum_ref[...] = jnp.zeros_like(sum_ref)
    total = total_ref[0]
    copy.wait()

    def add(group, carry):
        for part in range(unrolled):
            near, _, brick, tile, _ = entry(tiles_ref, group * unrolled + part, total)
            places = [ghost_ref[brick, c, pl.ds(tile, 1), :] for c in range(3)]
            factors, summed = far_factors(places, ghost_ref[brick, 3, pl.ds(tile, 1), :])
            both = dot(near_ref[near], factors, nn_dims)
            shrink = jnp.maximum(both[0:128], 0.0)
            weight = shrink * shrink * both[128:256]
            twice = jnp.concatenate([summed, summed], axis=1)
            sum_ref[near] += dot(twice, halves(weight), nt_dims)
        return carry

    lax.fori_loop(0, (total + unrolled - 1) // unrolled, add, 0)
    for c in range(3):
        for t in range(8):
            found = sum_ref[t]
            there = found[c : c + 1] + found[c + 4 : c + 5] + found[c + 8 : c + 9]
            here = own[c][t : t + 1] * found[3:4]
            push_ref[c, t : t + 1, :] = (-cutoff * cube_factor) * (here - there)


def force_pack_kernel(
    step,
    total_ref,
    tiles_in,
    c0,
    c1,
    c2,
    s0,
    s1,
    s2,
    own_slope,
    place_in,
    speed_in,
    slots_ref,
    place_ref,
    speed_ref,
    p0,
    p1,
    p2,
    p3,
    tiles_ref,
    ghost_ref,
    near_ref,
    sum_ref,
    push_ref,
    sem,
):
    force_sums(
        total_ref,
        tiles_in,
        (c0, c1, c2),
        (s0, s1, s2),
        own_slope,
        tiles_ref,
        ghost_ref,
        near_ref,
        sum_ref,
        push_ref,
        sem,
    )
    push = [push_ref[c] for c in range(3)]
    speed = [speed_in[c] + kick * push[c] for c in range(3)]
    drift_and_pack(
        [place_in[c] for c in range(3)],
        speed,
        push,
        slots_ref.at[step],
        place_ref,
        speed_ref,
        (p0, p1, p2, p3),
    )


def force_last_kernel(
    total_ref,
    tiles_in,
    c0,
    c1,
    c2,
    s0,
    s1,
    s2,
    own_slope,
    speed_in,
    speed_ref,
    tiles_ref,
    ghost_ref,
    near_ref,
    sum_ref,
    push_ref,
    sem,
):
    force_sums(
        total_ref,
        tiles_in,
        (c0, c1, c2),
        (s0, s1, s2),
        own_slope,
        tiles_ref,
        ghost_ref,
        near_ref,
        sum_ref,
        push_ref,
        sem,
    )
    for c in range(3):
        speed_ref[c] = speed_in[c] + kick * push_ref[c]


def pick_kernel(plane_ref, column_ref):
    count = lax.axis_size("gx")
    xbrick = lax.axis_index("gx")
    for dx in range(3):
        at = lax.rem(xbrick + (dx - 1 + count), count)
        for level in range(4):
            column_ref[dx * 4 + level] = plane_ref[at * 4 + level]


def shaped(*extent):
    return jax.ShapeDtypeStruct(extent, jnp.float32)


def call(kernel, outs, specs, scratch=()):
    return pl.pallas_call(
        kernel,
        out_shape=outs,
        in_specs=specs,
        out_specs=[VMEM] * len(outs),
        scratch_shapes=list(scratch),
        compiler_params=params,
    )


def moved(values, axis, shift):
    count = lax.axis_size(axis)
    return lax.ppermute(values, axis, [((i + shift) % count, i) for i in range(count)])


def migrants(packed):
    return (
        moved(packed[1], "gx", 1),
        moved(packed[0], "gx", -1),
        moved(packed[3], "gy", 1),
        moved(packed[2], "gy", -1),
    )


def around(values):
    rows = jnp.stack([moved(values, "gy", -1), values, moved(values, "gy", 1)])
    copies = jnp.broadcast_to(rows[None], (4,) + rows.shape)
    tower = lax.all_to_all(copies, "gz", 0, 0, tiled=True)
    return moved(tower, "gx", -1), tower, moved(tower, "gx", 1)


def slopes_around(values):
    count = lax.axis_size("gx") * lax.axis_size("gz")
    copies = jnp.broadcast_to(values[None], (count,) + values.shape)
    plane = lax.all_to_all(copies, ("gx", "gz"), 0, 0, tiled=True)
    (column,) = call(pick_kernel, [shaped(12, 8, 128)], [VMEM])(plane)
    return moved(column, "gy", -1), column, moved(column, "gy", 1)


def per_device(positions, velocities, forces, counts, pair_tiles, pair_count, mig_slots):
    live_count = counts.reshape(1)
    total = pair_count.reshape(1)
    tiles = pair_tiles.reshape(2, 128)
    steps = mig_slots.shape[0]
    slots = mig_slots.reshape(steps, 4, 128)
    atoms = shaped(3, 8, 128)
    block = shaped(8, 128)
    atoms_scratch = pltpu.VMEM((3, 8, 128), jnp.float32)

    def pair_scratch(comps, near_rows, sum_rows, found):
        return (
            pltpu.SMEM((2, 128), jnp.int32),
            pltpu.VMEM((37, comps, 8, 128), jnp.float32),
            pltpu.VMEM((8, near_rows, 32), jnp.bfloat16),
            pltpu.VMEM((8, sum_rows, 128), jnp.float32),
            found,
            pltpu.SemaphoreType.DMA,
        )

    place, speed, *packed, slots = call(
        pack_kernel,
        [atoms, atoms] + [block] * 4 + [jax.ShapeDtypeStruct(slots.shape, jnp.int32)],
        [ANY] * 4,
        (atoms_scratch, atoms_scratch, atoms_scratch, pltpu.SemaphoreType.DMA((4,))),
    )(
        positions.reshape(3, 8, 128),
        velocities.reshape(3, 8, 128),
        forces.reshape(3, 8, 128),
        slots,
    )
    for n in range(steps):
        place, speed, sent = call(
            functools.partial(unpack_kernel, n), [atoms, atoms, atoms], [SMEM] + [VMEM] * 7
        )(live_count, place, speed, slots, *migrants(packed))
        cells = around(sent)
        (slope,) = call(
            density_kernel,
            [block],
            [SMEM, ANY] + [VMEM] * 3,
            pair_scratch(3, 128, 128, pltpu.VMEM((8, 128), jnp.float32)),
        )(total, tiles, *cells)
        slope_cells = slopes_around(slope)
        scratch = pair_scratch(4, 256, 16, atoms_scratch)
        if n + 1 < steps:
            place, speed, *packed = call(
                functools.partial(force_pack_kernel, n + 1),
                [atoms, atoms] + [block] * 4,
                [SMEM, ANY] + [VMEM] * 10,
                scratch,
            )(total, tiles, *cells, *slope_cells, slope, place, speed, slots)
        else:
            (speed,) = call(
                force_last_kernel, [atoms], [SMEM, ANY] + [VMEM] * 8, scratch
            )(total, tiles, *cells, *slope_cells, slope, speed)
    return (place.reshape(positions.shape), speed.reshape(velocities.shape))


def solution(mesh):
    placed = (
        P(None, "gx", "gy", "gz", None),
        P(None, "gx", "gy", "gz", None),
        P(None, "gx", "gy", "gz", None),
        P("gx", "gy", "gz"),
        P(None, "gx", "gy", "gz", None),
        P("gx", "gy", "gz"),
        P(None, None, "gx", "gy", "gz", None),
    )
    return jax.shard_map(
        per_device,
        mesh=mesh,
        in_specs=placed,
        out_specs=(P(None, "gx", "gy", "gz", None), P(None, "gx", "gy", "gz", None)),
        check_vma=False,
    )
```

```python
import functools

import jax
import jax.numpy as jnp
from jax import lax
from jax.experimental import pallas as pl
from jax.experimental.pallas import tpu as pltpu
from jax.sharding import PartitionSpec as P

cutoff_sq = 0.81
cutoff = 0.9
height_ratio = 0.25
density_scale = 1.0 / 256.0
repulsion = 1.0 / 512.0
time_step = 0.25
kick = 0.5 * time_step
flat_scale = 1.0 / cutoff
tall_scale = height_ratio / cutoff
cube_factor = -8.0 * repulsion / cutoff_sq
slope_factor = -6.0 * density_scale / cutoff_sq
far_away = 1e15

VMEM = pl.BlockSpec(memory_space=pltpu.VMEM)
ANY = pl.BlockSpec(memory_space=pl.ANY)
SMEM = pl.BlockSpec(memory_space=pltpu.SMEM)
unrolled = 4
nt_dims = (((1,), (1,)), ((), ()))
nn_dims = (((1,), (0,)), ((), ()))


def dot(left, right, dims):
    return lax.dot_general(left, right, dims, preferred_element_type=jnp.float32)


def pieces(values, count):
    out = []
    for _ in range(count):
        part = values.astype(jnp.bfloat16)
        out.append(part)
        values = values - part.astype(jnp.float32)
    return out


def slot_masks(slots_ref, direction):
    slots = slots_ref[direction : direction + 1, :]
    lane_hit = lax.broadcasted_iota(jnp.int32, (128, 128), 0) == (slots & 127)
    tile_hit = lax.broadcasted_iota(jnp.int32, (8, 128), 0) == (slots >> 7)
    return jnp.where(lane_hit, 1.0, 0.0).astype(jnp.bfloat16), tile_hit


def drift_and_pack(place, speed, push, slots_ref, place_ref, speed_ref, packed_refs):
    speed = [speed[c] + kick * push[c] for c in range(3)]
    rates = (time_step, time_step, time_step / height_ratio)
    place = [place[c] + rates[c] * speed[c] for c in range(3)]
    for c in range(3):
        place_ref[c] = place[c]
        speed_ref[c] = speed[c]
    rows = jnp.concatenate(place + speed, axis=0)
    split = jnp.concatenate(pieces(rows, 3), axis=0)
    for direction in range(4):
        lane_hit, tile_hit = slot_masks(slots_ref, direction)
        found = dot(split, lane_hit, nn_dims)
        found = found[0:48] + found[48:96] + found[96:144]
        for c in range(6):
            chosen = jnp.where(tile_hit, found[8 * c : 8 * c + 8], 0.0)
            packed_refs[direction][c : c + 1, :] = jnp.sum(chosen, axis=0, keepdims=True)
        packed_refs[direction][6:8, :] = jnp.zeros((2, 128), jnp.float32)


def put_plan(total, tiles, plan_ref, selves_ref):
    zbrick = lax.axis_index("gz")
    near = tiles[0:1]
    far = tiles[1:2]
    lanes = lax.broadcasted_iota(jnp.int32, (1, 128), 1)
    near = jnp.where(lanes < total, near, -1)
    rows = lax.broadcasted_iota(jnp.int32, (16, 128), 0)
    mine = jnp.where(rows == near, 1.0, 0.0)
    before = lax.broadcasted_iota(jnp.int32, (128, 128), 0) < lax.broadcasted_iota(
        jnp.int32, (128, 128), 1
    )
    ones = jnp.ones((128, 128), jnp.bfloat16)
    rank = dot(mine.astype(jnp.bfloat16), jnp.where(before, 1.0, 0.0).astype(jnp.bfloat16), nn_dims)
    count = dot(mine.astype(jnp.bfloat16), ones, nn_dims)
    itself = jnp.where(far == (16 + zbrick) * 8 + near, mine, 0.0)
    selves_ref[...] = dot(itself.astype(jnp.bfloat16), ones, nn_dims)[0:8]
    groups = (count.astype(jnp.int32) + (unrolled - 1)) // unrolled
    place = jnp.full((1, 128), -1, jnp.int32)
    start = jnp.zeros((1, 128), jnp.int32)
    starts = jnp.zeros((1, 128), jnp.int32)
    for t in range(8):
        at = start * unrolled + rank[t : t + 1].astype(jnp.int32)
        place = jnp.where(near == t, at, place)
        starts = jnp.where(lanes == t, start, starts)
        start = start + groups[t : t + 1]
    starts = jnp.where(lanes == 8, start, starts)
    values = jnp.where(
        rows == 0,
        (far >> 3).astype(jnp.float32),
        jnp.where(rows == 1, (far & 7).astype(jnp.float32), 1.0),
    ).astype(jnp.bfloat16)
    for half in range(2):
        spot = lax.broadcasted_iota(jnp.int32, (128, 128), 0) + 128 * half
        sent = jnp.where(spot == place, 1.0, 0.0).astype(jnp.bfloat16)
        sorted_rows = dot(values, sent, nt_dims).astype(jnp.int32)
        brick = jnp.where(sorted_rows[2:3] > 0, sorted_rows[0:1], 36)
        plan_ref[half : half + 1, :] = brick * 8 + sorted_rows[1:2]
    plan_ref[2:3, :] = starts
    plan_ref[3:8, :] = jnp.zeros((5, 128), jnp.int32)


def pack_kernel(
    total_ref,
    place_in,
    speed_in,
    push_in,
    slots_in,
    tiles_in,
    place_ref,
    speed_ref,
    p0,
    p1,
    p2,
    p3,
    slots_out,
    plan_ref,
    selves_ref,
    place_at,
    speed_at,
    push_at,
    tiles_at,
    sems,
):
    pairs = (
        (place_in, place_at),
        (speed_in, speed_at),
        (push_in, push_at),
        (slots_in, slots_out),
        (tiles_in, tiles_at),
    )
    copies = [
        pltpu.make_async_copy(here, there, sems.at[i]) for i, (here, there) in enumerate(pairs)
    ]
    for copy in copies:
        copy.start()
    for copy in copies:
        copy.wait()
    drift_and_pack(
        [place_at[c] for c in range(3)],
        [speed_at[c] for c in range(3)],
        [push_at[c] for c in range(3)],
        slots_out.at[0],
        place_ref,
        speed_ref,
        (p0, p1, p2, p3),
    )
    put_plan(total_ref[0], tiles_at[...], plan_ref, selves_ref)


def unpack_kernel(
    step, count_ref, place_in, speed_in, slots_in, a0, a1, a2, a3, place_ref, speed_ref, sent_ref
):
    slots_ref = slots_in.at[step]
    total = jnp.zeros((160, 128), jnp.float32)
    plan = ((a0, 0, 1.0), (a1, 0, -1.0), (a2, 1, 1.0), (a3, 1, -1.0))
    for direction, (arrived, component, shift) in enumerate(plan):
        lane_hit, tile_hit = slot_masks(slots_ref, direction)
        rows = []
        for c in range(6):
            row = arrived[c : c + 1, :]
            if c == component:
                row = row + shift
            rows.append(jnp.where(tile_hit, row, 0.0))
        marks = jnp.where(tile_hit, 1.0, 0.0)
        split = pieces(jnp.concatenate(rows, axis=0), 3)
        split.append(jnp.concatenate([marks, jnp.zeros_like(marks)], axis=0).astype(jnp.bfloat16))
        total = total + dot(jnp.concatenate(split, axis=0), lane_hit, nt_dims)
    put = total[0:48] + total[48:96] + total[96:144]
    taken = total[144:152] > 0.5
    slot_ids = lax.broadcasted_iota(jnp.int32, (8, 128), 0) * 128 + lax.broadcasted_iota(
        jnp.int32, (8, 128), 1
    )
    live = slot_ids < count_ref[0]
    scales = (flat_scale, flat_scale, tall_scale)
    for c in range(3):
        place = jnp.where(taken, put[8 * c : 8 * c + 8], place_in[c])
        place_ref[c] = place
        speed_ref[c] = jnp.where(taken, put[24 + 8 * c : 32 + 8 * c], speed_in[c])
        sent_ref[c] = jnp.where(live, place * scales[c], far_away)


def put_ghosts(cells, ghost_ref):
    zbrick = lax.axis_index("gz")
    for level in range(4):
        rise = ((level - zbrick).astype(jnp.float32) - 0.5) * tall_scale
        for dx, cell in enumerate(cells):
            for dy in range(3):
                brick = dx * 12 + dy * 4 + level
                ghost_ref[brick, 0] = cell[level, dy, 0] + (dx - 1.5) * flat_scale
                ghost_ref[brick, 1] = cell[level, dy, 1] + (dy - 1.5) * flat_scale
                ghost_ref[brick, 2] = cell[level, dy, 2] + rise
    ghost_ref[36] = jnp.full(ghost_ref.shape[1:], far_away, jnp.float32)


def own_places(middle):
    zbrick = lax.axis_index("gz")
    own = [middle[zbrick, 1, c] for c in range(3)]
    live = own[0] < 0.5 * far_away
    shifts = (0.5 * flat_scale, 0.5 * flat_scale, 0.5 * tall_scale)
    return [jnp.where(live, row - shift, -far_away) for row, shift in zip(own, shifts)], live


def put_columns(rows, column_ref):
    turned = jnp.concatenate(rows, axis=0).T
    for at in range(8 * len(rows)):
        column_ref[at] = jnp.broadcast_to(turned[:, at : at + 1], (128, 128))


def row_sums(block):
    first = block.astype(jnp.bfloat16)
    second = (block - first.astype(jnp.float32)).astype(jnp.bfloat16)
    split = jnp.concatenate([first, second], axis=1)
    sums = dot(split, jnp.ones((256, 128), jnp.bfloat16), nn_dims)
    on_line = lax.broadcasted_iota(jnp.int32, (128, 128), 0) == lax.broadcasted_iota(
        jnp.int32, (128, 128), 1
    )
    return jnp.sum(jnp.where(on_line, sums, 0.0), axis=0, keepdims=True)


def over_entries(plan_ref, body):
    def over_tile(near, carry):
        def over_group(group, carry):
            first = group * unrolled
            codes = [plan_ref[(first + i) >> 7, (first + i) & 127] for i in range(unrolled)]
            body(near, [(code >> 3, code & 7) for code in codes])
            return carry

        return lax.fori_loop(plan_ref[2, near], plan_ref[2, near + 1], over_group, carry)

    lax.fori_loop(0, 8, over_tile, 0)


def density_kernel(
    plan_in,
    selves_ref,
    behind,
    middle,
    ahead,
    slope_ref,
    plan_ref,
    ghost_ref,
    column_ref,
    sum_ref,
    row_ref,
    sem,
):
    copy = pltpu.make_async_copy(plan_in, plan_ref, sem)
    copy.start()
    put_ghosts((behind, middle, ahead), ghost_ref)
    own, live = own_places(middle)
    rest = 0.5 - (own[0] * own[0] + own[1] * own[1] + own[2] * own[2])
    put_columns([2.0 * row for row in own] + [rest], column_ref)
    sum_ref[...] = jnp.zeros_like(sum_ref)
    copy.wait()

    def add(near, ghosts):
        far = []
        for brick, tile in ghosts:
            x, y, z = (ghost_ref[brick, c, pl.ds(tile, 1), :] for c in range(3))
            rows = (x, y, z, 0.5 - (x * x + y * y + z * z))
            far.append([jnp.broadcast_to(row, (8, 128)) for row in rows])
        for r in range(16):
            part = pl.ds(8 * r, 8)
            ax, ay, az, rest = (column_ref[8 * c + near, part, :] for c in range(4))
            total = sum_ref[near, part, :]
            for cx, cy, cz, cn in far:
                shrink = jnp.maximum((ax * cx + ay * cy) + (az * cz + (rest + cn)), 0.0)
                total = total + shrink * shrink * shrink
            sum_ref[near, part, :] = total

    over_entries(plan_ref, add)
    for t in range(8):
        row_ref[t : t + 1, :] = row_sums(sum_ref[t])
    density = (row_ref[...] - jnp.where(live, selves_ref[...], 0.0)) * density_scale
    slope_ref[...] = (-0.5 * slope_factor / cube_factor) / jnp.sqrt(1.0 + density)


def force_sums(
    plan_in,
    cells,
    slope_cells,
    own_slope,
    plan_ref,
    ghost_ref,
    column_ref,
    sum_ref,
    push_ref,
    sem,
):
    copy = pltpu.make_async_copy(plan_in, plan_ref, sem)
    copy.start()
    put_ghosts(cells, ghost_ref)
    for dy, cell in enumerate(slope_cells):
        for dx in range(3):
            for level in range(4):
                ghost_ref[dx * 12 + dy * 4 + level, 3] = cell[dx * 4 + level]
    own, _ = own_places(cells[1])
    put_columns(own + [own_slope[...]], column_ref)
    sum_ref[...] = jnp.zeros_like(sum_ref)
    copy.wait()

    def add(near, ghosts):
        far = []
        for brick, tile in ghosts:
            rows = [ghost_ref[brick, c, pl.ds(tile, 1), :] for c in range(4)]
            far.append([jnp.broadcast_to(row, (8, 128)) for row in rows])
        for r in range(16):
            part = pl.ds(8 * r, 8)
            ax, ay, az, slope = (column_ref[8 * c + near, part, :] for c in range(4))
            sums = [sum_ref[8 * c + near, part, :] for c in range(3)]
            for cx, cy, cz, far_slope in far:
                dx = ax - cx
                dy = ay - cy
                dz = az - cz
                shrink = jnp.maximum(1.0 - (dx * dx + dy * dy + dz * dz), 0.0)
                weight = shrink * shrink * (shrink + (slope + far_slope))
                sums = [sums[0] + weight * dx, sums[1] + weight * dy, sums[2] + weight * dz]
            for c in range(3):
                sum_ref[8 * c + near, part, :] = sums[c]

    over_entries(plan_ref, add)
    for c in range(3):
        for t in range(8):
            push_ref[c, t : t + 1, :] = (-cutoff * cube_factor) * row_sums(sum_ref[8 * c + t])


def force_pack_kernel(
    step,
    plan_in,
    c0,
    c1,
    c2,
    s0,
    s1,
    s2,
    own_slope,
    place_in,
    speed_in,
    slots_ref,
    place_ref,
    speed_ref,
    p0,
    p1,
    p2,
    p3,
    plan_ref,
    ghost_ref,
    column_ref,
    sum_ref,
    push_ref,
    sem,
):
    force_sums(
        plan_in,
        (c0, c1, c2),
        (s0, s1, s2),
        own_slope,
        plan_ref,
        ghost_ref,
        column_ref,
        sum_ref,
        push_ref,
        sem,
    )
    push = [push_ref[c] for c in range(3)]
    speed = [speed_in[c] + kick * push[c] for c in range(3)]
    drift_and_pack(
        [place_in[c] for c in range(3)],
        speed,
        push,
        slots_ref.at[step],
        place_ref,
        speed_ref,
        (p0, p1, p2, p3),
    )


def force_last_kernel(
    plan_in,
    c0,
    c1,
    c2,
    s0,
    s1,
    s2,
    own_slope,
    speed_in,
    speed_ref,
    plan_ref,
    ghost_ref,
    column_ref,
    sum_ref,
    push_ref,
    sem,
):
    force_sums(
        plan_in,
        (c0, c1, c2),
        (s0, s1, s2),
        own_slope,
        plan_ref,
        ghost_ref,
        column_ref,
        sum_ref,
        push_ref,
        sem,
    )
    for c in range(3):
        speed_ref[c] = speed_in[c] + kick * push_ref[c]


def pick_kernel(plane_ref, column_ref):
    count = lax.axis_size("gx")
    xbrick = lax.axis_index("gx")
    for dx in range(3):
        at = lax.rem(xbrick + (dx - 1 + count), count)
        for level in range(4):
            column_ref[dx * 4 + level] = plane_ref[at * 4 + level]


def shaped(*extent):
    return jax.ShapeDtypeStruct(extent, jnp.float32)


def call(kernel, outs, specs, scratch=(), mebibytes=24):
    return pl.pallas_call(
        kernel,
        out_shape=outs,
        in_specs=specs,
        out_specs=[VMEM] * len(outs),
        scratch_shapes=list(scratch),
        compiler_params=pltpu.CompilerParams(vmem_limit_bytes=mebibytes * 2**20),
    )


def moved(values, axis, shift):
    count = lax.axis_size(axis)
    return lax.ppermute(values, axis, [((i + shift) % count, i) for i in range(count)])


def migrants(packed):
    return (
        moved(packed[1], "gx", 1),
        moved(packed[0], "gx", -1),
        moved(packed[3], "gy", 1),
        moved(packed[2], "gy", -1),
    )


def around(values):
    rows = jnp.stack([moved(values, "gy", -1), values, moved(values, "gy", 1)])
    copies = jnp.broadcast_to(rows[None], (4,) + rows.shape)
    tower = lax.all_to_all(copies, "gz", 0, 0, tiled=True)
    return moved(tower, "gx", -1), tower, moved(tower, "gx", 1)


def slopes_around(values):
    count = lax.axis_size("gx") * lax.axis_size("gz")
    copies = jnp.broadcast_to(values[None], (count,) + values.shape)
    plane = lax.all_to_all(copies, ("gx", "gz"), 0, 0, tiled=True)
    (column,) = call(pick_kernel, [shaped(12, 8, 128)], [VMEM])(plane)
    return moved(column, "gy", -1), column, moved(column, "gy", 1)


def per_device(positions, velocities, forces, counts, pair_tiles, pair_count, mig_slots):
    live_count = counts.reshape(1)
    total = pair_count.reshape(1)
    tiles = pair_tiles.reshape(2, 128)
    steps = mig_slots.shape[0]
    slots = mig_slots.reshape(steps, 4, 128)
    atoms = shaped(3, 8, 128)
    block = shaped(8, 128)
    atoms_scratch = pltpu.VMEM((3, 8, 128), jnp.float32)

    plan_shape = jax.ShapeDtypeStruct((8, 128), jnp.int32)

    def pair_scratch(columns, sums, found):
        return (
            pltpu.SMEM((8, 128), jnp.int32),
            pltpu.VMEM((37, columns, 8, 128), jnp.float32),
            pltpu.VMEM((8 * columns, 128, 128), jnp.float32),
            pltpu.VMEM((8 * sums, 128, 128), jnp.float32),
            found,
            pltpu.SemaphoreType.DMA,
        )

    place, speed, p0, p1, p2, p3, slots, plan, selves = call(
        pack_kernel,
        [atoms, atoms]
        + [block] * 4
        + [jax.ShapeDtypeStruct(slots.shape, jnp.int32), plan_shape, block],
        [SMEM] + [ANY] * 5,
        (atoms_scratch,) * 3
        + (pltpu.VMEM((2, 128), jnp.int32), pltpu.SemaphoreType.DMA((5,))),
        56,
    )(
        total,
        positions.reshape(3, 8, 128),
        velocities.reshape(3, 8, 128),
        forces.reshape(3, 8, 128),
        slots,
        tiles,
    )
    packed = p0, p1, p2, p3
    for n in range(steps):
        place, speed, sent = call(
            functools.partial(unpack_kernel, n), [atoms, atoms, atoms], [SMEM] + [VMEM] * 7
        )(live_count, place, speed, slots, *migrants(packed))
        cells = around(sent)
        (slope,) = call(
            density_kernel,
            [block],
            [ANY] + [VMEM] * 4,
            pair_scratch(4, 1, pltpu.VMEM((8, 128), jnp.float32)),
        )(plan, selves, *cells)
        slope_cells = slopes_around(slope)
        scratch = pair_scratch(4, 3, atoms_scratch)
        if n + 1 < steps:
            place, speed, *packed = call(
                functools.partial(force_pack_kernel, n + 1),
                [atoms, atoms] + [block] * 4,
                [ANY] + [VMEM] * 10,
                scratch,
            )(plan, *cells, *slope_cells, slope, place, speed, slots)
        else:
            (speed,) = call(force_last_kernel, [atoms], [ANY] + [VMEM] * 8, scratch)(
                plan, *cells, *slope_cells, slope, speed
            )
    return (place.reshape(positions.shape), speed.reshape(velocities.shape))


def solution(mesh):
    placed = (
        P(None, "gx", "gy", "gz", None),
        P(None, "gx", "gy", "gz", None),
        P(None, "gx", "gy", "gz", None),
        P("gx", "gy", "gz"),
        P(None, "gx", "gy", "gz", None),
        P("gx", "gy", "gz"),
        P(None, None, "gx", "gy", "gz", None),
    )
    return jax.shard_map(
        per_device,
        mesh=mesh,
        in_specs=placed,
        out_specs=(P(None, "gx", "gy", "gz", None), P(None, "gx", "gy", "gz", None)),
        check_vma=False,
    )
```

```python
import functools

import jax
import jax.numpy as jnp
from jax import lax
from jax.experimental import pallas as pl
from jax.experimental.pallas import tpu as pltpu
from jax.sharding import PartitionSpec as P

cutoff_sq = 0.81
cutoff = 0.9
height_ratio = 0.25
density_scale = 1.0 / 256.0
repulsion = 1.0 / 512.0
time_step = 0.25
kick = 0.5 * time_step
flat_scale = 1.0 / cutoff
tall_scale = height_ratio / cutoff
cube_factor = -8.0 * repulsion / cutoff_sq
slope_factor = -6.0 * density_scale / cutoff_sq
far_away = 1e15

VMEM = pl.BlockSpec(memory_space=pltpu.VMEM)
ANY = pl.BlockSpec(memory_space=pl.ANY)
SMEM = pl.BlockSpec(memory_space=pltpu.SMEM)
unrolled = 4
nt_dims = (((1,), (1,)), ((), ()))
nn_dims = (((1,), (0,)), ((), ()))


def dot(left, right, dims):
    return lax.dot_general(left, right, dims, preferred_element_type=jnp.float32)


def pieces(values, count):
    out = []
    for _ in range(count):
        part = values.astype(jnp.bfloat16)
        out.append(part)
        values = values - part.astype(jnp.float32)
    return out


def slot_masks(slots_ref, direction):
    slots = slots_ref[direction : direction + 1, :]
    lane_hit = lax.broadcasted_iota(jnp.int32, (128, 128), 0) == (slots & 127)
    tile_hit = lax.broadcasted_iota(jnp.int32, (8, 128), 0) == (slots >> 7)
    return jnp.where(lane_hit, 1.0, 0.0).astype(jnp.bfloat16), tile_hit


def drift_and_pack(place, speed, push, slots_ref, place_ref, speed_ref, packed_refs):
    speed = [speed[c] + kick * push[c] for c in range(3)]
    rates = (time_step, time_step, time_step / height_ratio)
    place = [place[c] + rates[c] * speed[c] for c in range(3)]
    for c in range(3):
        place_ref[c] = place[c]
        speed_ref[c] = speed[c]
    rows = jnp.concatenate(place + speed, axis=0)
    split = jnp.concatenate(pieces(rows, 3), axis=0)
    for direction in range(4):
        lane_hit, tile_hit = slot_masks(slots_ref, direction)
        found = dot(split, lane_hit, nn_dims)
        found = found[0:48] + found[48:96] + found[96:144]
        for c in range(6):
            chosen = jnp.where(tile_hit, found[8 * c : 8 * c + 8], 0.0)
            packed_refs[direction][c : c + 1, :] = jnp.sum(chosen, axis=0, keepdims=True)
        packed_refs[direction][6:8, :] = jnp.zeros((2, 128), jnp.float32)


def put_plan(listed, near, far, late, plan_ref):
    lanes = lax.broadcasted_iota(jnp.int32, (1, 128), 1)
    part = jnp.where(listed, jnp.where(late, near + 8, near), -1)
    rows = lax.broadcasted_iota(jnp.int32, (16, 128), 0)
    mine = jnp.where(rows == part, 1.0, 0.0).astype(jnp.bfloat16)
    before = lax.broadcasted_iota(jnp.int32, (128, 128), 0) < lax.broadcasted_iota(
        jnp.int32, (128, 128), 1
    )
    rank = dot(mine, jnp.where(before, 1.0, 0.0).astype(jnp.bfloat16), nn_dims)
    count = dot(mine, jnp.ones((128, 128), jnp.bfloat16), nn_dims)
    groups = (count.astype(jnp.int32) + (unrolled - 1)) // unrolled
    place = jnp.full((1, 128), -1, jnp.int32)
    start = jnp.zeros((1, 128), jnp.int32)
    starts = jnp.zeros((1, 128), jnp.int32)
    for t in range(16):
        at = start * unrolled + rank[t : t + 1].astype(jnp.int32)
        place = jnp.where(part == t, at, place)
        starts = jnp.where(lanes == t, start, starts)
        start = start + groups[t : t + 1]
    starts = jnp.where(lanes == 16, start, starts)
    values = jnp.where(
        rows == 0,
        (far >> 3).astype(jnp.float32),
        jnp.where(rows == 1, (far & 7).astype(jnp.float32), 1.0),
    ).astype(jnp.bfloat16)
    for half in range(2):
        spot = lax.broadcasted_iota(jnp.int32, (128, 128), 0) + 128 * half
        sent = jnp.where(spot == place, 1.0, 0.0).astype(jnp.bfloat16)
        sorted_rows = dot(values, sent, nt_dims).astype(jnp.int32)
        brick = jnp.where(sorted_rows[2:3] > 0, sorted_rows[0:1], 36)
        plan_ref[half : half + 1, :] = brick * 8 + sorted_rows[1:2]
    plan_ref[2:3, :] = starts
    plan_ref[3:8, :] = jnp.zeros((5, 128), jnp.int32)


def plan_kernel(total_ref, count_ref, tiles_ref, density_plan, force_plan, selves_ref):
    zbrick = lax.axis_index("gz")
    near = tiles_ref[0:1, :]
    far = tiles_ref[1:2, :]
    listed = lax.broadcasted_iota(jnp.int32, (1, 128), 1) < total_ref[0]
    listed = jnp.logical_and(listed, near * 128 < count_ref[0])
    brick = far >> 3
    put_plan(listed, near, far, jnp.logical_or(brick < 12, brick >= 24), density_plan)
    put_plan(listed, near, far, ((brick >> 2) + 2) % 3 != 0, force_plan)
    rows = lax.broadcasted_iota(jnp.int32, (16, 128), 0)
    itself = jnp.logical_and(listed, far == (16 + zbrick) * 8 + near)
    itself = jnp.where(jnp.logical_and(itself, rows == near), 1.0, 0.0).astype(jnp.bfloat16)
    selves_ref[...] = dot(itself, jnp.ones((128, 128), jnp.bfloat16), nn_dims)[0:8]


def pack_kernel(rows_in, slots_in, place_ref, speed_ref, slots_out, *packed_refs):
    slots_out[...] = slots_in[...]
    drift_and_pack(
        [rows_in[c] for c in range(3)],
        [rows_in[c + 3] for c in range(3)],
        [rows_in[c + 6] for c in range(3)],
        slots_in.at[0],
        place_ref,
        speed_ref,
        packed_refs,
    )


def unpack_kernel(
    step, count_ref, place_in, speed_in, slots_in, a0, a1, a2, a3, place_ref, speed_ref, sent_ref
):
    slots_ref = slots_in.at[step]
    total = jnp.zeros((160, 128), jnp.float32)
    plan = ((a0, 0, 1.0), (a1, 0, -1.0), (a2, 1, 1.0), (a3, 1, -1.0))
    for direction, (arrived, component, shift) in enumerate(plan):
        lane_hit, tile_hit = slot_masks(slots_ref, direction)
        rows = []
        for c in range(6):
            row = arrived[c : c + 1, :]
            if c == component:
                row = row + shift
            rows.append(jnp.where(tile_hit, row, 0.0))
        marks = jnp.where(tile_hit, 1.0, 0.0)
        split = pieces(jnp.concatenate(rows, axis=0), 3)
        split.append(jnp.concatenate([marks, jnp.zeros_like(marks)], axis=0).astype(jnp.bfloat16))
        total = total + dot(jnp.concatenate(split, axis=0), lane_hit, nt_dims)
    put = total[0:48] + total[48:96] + total[96:144]
    taken = total[144:152] > 0.5
    slot_ids = lax.broadcasted_iota(jnp.int32, (8, 128), 0) * 128 + lax.broadcasted_iota(
        jnp.int32, (8, 128), 1
    )
    live = slot_ids < count_ref[0]
    scales = (flat_scale, flat_scale, tall_scale)
    for c in range(3):
        place = jnp.where(taken, put[8 * c : 8 * c + 8], place_in[c])
        place_ref[c] = place
        speed_ref[c] = jnp.where(taken, put[24 + 8 * c : 32 + 8 * c], speed_in[c])
        sent_ref[c] = jnp.where(live, place * scales[c], far_away)


def put_ghosts(cells, ghost_ref, wanted):
    zbrick = lax.axis_index("gz")
    for level in range(4):
        rise = ((level - zbrick).astype(jnp.float32) - 0.5) * tall_scale
        for dx, cell in enumerate(cells):
            for dy in range(3):
                if not wanted(dx, dy):
                    continue
                brick = dx * 12 + dy * 4 + level
                ghost_ref[brick, 0] = cell[level, dy, 0] + (dx - 1.5) * flat_scale
                ghost_ref[brick, 1] = cell[level, dy, 1] + (dy - 1.5) * flat_scale
                ghost_ref[brick, 2] = cell[level, dy, 2] + rise
    ghost_ref[36] = jnp.full(ghost_ref.shape[1:], far_away, jnp.float32)


def own_places(middle):
    zbrick = lax.axis_index("gz")
    own = [middle[zbrick, 1, c] for c in range(3)]
    live = own[0] < 0.5 * far_away
    shifts = (0.5 * flat_scale, 0.5 * flat_scale, 0.5 * tall_scale)
    return [jnp.where(live, row - shift, -far_away) for row, shift in zip(own, shifts)], live


def put_columns(rows, column_ref):
    turned = jnp.concatenate(rows, axis=0).T
    for at in range(8 * len(rows)):
        column_ref[at] = jnp.broadcast_to(turned[:, at : at + 1], (128, 128))


def row_sums(block):
    first = block.astype(jnp.bfloat16)
    second = (block - first.astype(jnp.float32)).astype(jnp.bfloat16)
    split = jnp.concatenate([first, second], axis=1)
    sums = dot(split, jnp.ones((256, 128), jnp.bfloat16), nn_dims)
    on_line = lax.broadcasted_iota(jnp.int32, (128, 128), 0) == lax.broadcasted_iota(
        jnp.int32, (128, 128), 1
    )
    return jnp.sum(jnp.where(on_line, sums, 0.0), axis=0, keepdims=True)


def over_entries(plan_in, plan_ref, sem, late, prepare, body):
    copy = pltpu.make_async_copy(plan_in, plan_ref, sem)
    copy.start()
    prepare()
    copy.wait()

    def over_tile(near, carry):
        def over_group(group, carry):
            first = group * unrolled
            codes = [plan_ref[(first + i) >> 7, (first + i) & 127] for i in range(unrolled)]
            body(near, [(code >> 3, code & 7) for code in codes])
            return carry

        segment = near + 8 * late
        return lax.fori_loop(plan_ref[2, segment], plan_ref[2, segment + 1], over_group, carry)

    lax.fori_loop(0, 8, over_tile, 0)


def density_sums(plan_in, cells, column_ref, late, plan_ref, ghost_ref, sum_ref, sem):
    def prepare():
        put_ghosts(cells, ghost_ref, lambda dx, dy: (dx != 1) == late)
        sum_ref[...] = jnp.zeros_like(sum_ref)

    def add(near, ghosts):
        far = []
        for brick, tile in ghosts:
            x, y, z = (ghost_ref[brick, c, pl.ds(tile, 1), :] for c in range(3))
            rows = (2.0 * x, 2.0 * y, 2.0 * z, 0.5 - (x * x + y * y + z * z))
            far.append([jnp.broadcast_to(row, (8, 128)) for row in rows])
        for r in range(16):
            part = pl.ds(8 * r, 8)
            ax, ay, az, rest = (column_ref[8 * c + near, part, :] for c in range(4))
            total = sum_ref[near, part, :]
            for cx, cy, cz, cn in far:
                shrink = jnp.maximum((ax * cx + ay * cy) + (az * cz + (rest + cn)), 0.0)
                total = total + shrink * shrink * shrink
            sum_ref[near, part, :] = total

    over_entries(plan_in, plan_ref, sem, late, prepare, add)


def early_density_kernel(
    plan_in, middle, column_ref, early_ref, plan_ref, ghost_ref, sum_ref, sem
):
    own, _ = own_places(middle)
    rest = 0.5 - (own[0] * own[0] + own[1] * own[1] + own[2] * own[2])
    put_columns(own + [rest], column_ref)
    cells = (None, middle, None)
    density_sums(plan_in, cells, column_ref, False, plan_ref, ghost_ref, sum_ref, sem)
    for t in range(8):
        early_ref[t : t + 1, :] = row_sums(sum_ref[t])


def late_density_kernel(
    plan_in,
    selves_ref,
    early_ref,
    column_ref,
    behind,
    middle,
    ahead,
    slope_ref,
    plan_ref,
    ghost_ref,
    sum_ref,
    row_ref,
    sem,
):
    cells = (behind, middle, ahead)
    density_sums(plan_in, cells, column_ref, True, plan_ref, ghost_ref, sum_ref, sem)
    for t in range(8):
        row_ref[t : t + 1, :] = row_sums(sum_ref[t])
    _, live = own_places(middle)
    itself = jnp.where(live, selves_ref[...], 0.0)
    density = (row_ref[...] + early_ref[...] - itself) * density_scale
    slope_ref[...] = (-0.5 * slope_factor / cube_factor) / jnp.sqrt(1.0 + density)


def force_sums(
    plan_in, cells, slope_cells, column_ref, slopes_ref, late, plan_ref, ghost_ref, sum_ref, sem
):
    def prepare():
        put_ghosts(cells, ghost_ref, lambda dx, dy: (dy != 1) == late)
        for dy, cell in enumerate(slope_cells):
            if (dy != 1) == late:
                for dx in range(3):
                    for level in range(4):
                        ghost_ref[dx * 12 + dy * 4 + level, 3] = cell[dx * 4 + level]
        sum_ref[...] = jnp.zeros_like(sum_ref)

    def add(near, ghosts):
        far = []
        for brick, tile in ghosts:
            rows = [ghost_ref[brick, c, pl.ds(tile, 1), :] for c in range(4)]
            far.append([jnp.broadcast_to(row, (8, 128)) for row in rows])
        for r in range(16):
            part = pl.ds(8 * r, 8)
            ax, ay, az = (column_ref[8 * c + near, part, :] for c in range(3))
            slope = slopes_ref[near, part, :]
            sums = [sum_ref[8 * c + near, part, :] for c in range(3)]
            for cx, cy, cz, far_slope in far:
                dx = ax - cx
                dy = ay - cy
                dz = az - cz
                shrink = jnp.maximum(1.0 - (dx * dx + dy * dy + dz * dz), 0.0)
                weight = shrink * shrink * (shrink + (slope + far_slope))
                sums = [sums[0] + weight * dx, sums[1] + weight * dy, sums[2] + weight * dz]
            for c in range(3):
                sum_ref[8 * c + near, part, :] = sums[c]

    over_entries(plan_in, plan_ref, sem, late, prepare, add)


def early_force_kernel(
    plan_in,
    c0,
    c1,
    c2,
    column_ref,
    own_slope,
    s1,
    slopes_ref,
    early_ref,
    plan_ref,
    ghost_ref,
    sum_ref,
    sem,
):
    put_columns([own_slope[...]], slopes_ref)
    force_sums(
        plan_in,
        (c0, c1, c2),
        (None, s1, None),
        column_ref,
        slopes_ref,
        False,
        plan_ref,
        ghost_ref,
        sum_ref,
        sem,
    )
    for c in range(3):
        for t in range(8):
            early_ref[c, t : t + 1, :] = row_sums(sum_ref[8 * c + t])


def late_force_kernel(
    step,
    plan_in,
    c0,
    c1,
    c2,
    column_ref,
    s0,
    s2,
    slopes_ref,
    early_ref,
    place_in,
    speed_in,
    *rest,
):
    *outs, plan_ref, ghost_ref, sum_ref, push_ref, sem = rest
    force_sums(
        plan_in,
        (c0, c1, c2),
        (s0, None, s2),
        column_ref,
        slopes_ref,
        True,
        plan_ref,
        ghost_ref,
        sum_ref,
        sem,
    )
    for c in range(3):
        for t in range(8):
            push_ref[c, t : t + 1, :] = row_sums(sum_ref[8 * c + t])
    push = [(-cutoff * cube_factor) * (push_ref[c] + early_ref[c]) for c in range(3)]
    place = [place_in[c] for c in range(3)]
    speed = [speed_in[c] + kick * push[c] for c in range(3)]
    if step is None:
        place_ref, speed_ref = outs
        for c in range(3):
            place_ref[c] = place[c]
            speed_ref[c] = speed[c]
    else:
        slots_ref, place_ref, speed_ref, *packed = outs
        drift_and_pack(place, speed, push, slots_ref.at[step], place_ref, speed_ref, packed)


def pick_kernel(plane_ref, column_ref):
    count = lax.axis_size("gx")
    xbrick = lax.axis_index("gx")
    for dx in range(3):
        at = lax.rem(xbrick + (dx - 1 + count), count)
        for level in range(4):
            column_ref[dx * 4 + level] = plane_ref[at * 4 + level]


def shaped(*extent):
    return jax.ShapeDtypeStruct(extent, jnp.float32)


def call(kernel, outs, specs, scratch=(), mega_ops=1):
    return pl.pallas_call(
        kernel,
        out_shape=outs,
        in_specs=specs,
        out_specs=[VMEM] * len(outs),
        scratch_shapes=list(scratch),
        compiler_params=pltpu.CompilerParams(vmem_limit_bytes=24 * 2**20),
        cost_estimate=pl.CostEstimate(
            flops=mega_ops * 10**6, bytes_accessed=mega_ops * 10**5, transcendentals=0
        ),
    )


def moved(values, axis, shift):
    count = lax.axis_size(axis)
    return lax.ppermute(values, axis, [((i + shift) % count, i) for i in range(count)])


def migrants(packed):
    return (
        moved(packed[1], "gx", 1),
        moved(packed[0], "gx", -1),
        moved(packed[3], "gy", 1),
        moved(packed[2], "gy", -1),
    )


def around(values, beside):
    ends, beside = lax.optimization_barrier(
        ((moved(values, "gy", -1), moved(values, "gy", 1)), beside)
    )
    rows = jnp.stack([ends[0], values, ends[1]])
    copies = jnp.broadcast_to(rows[None], (4,) + rows.shape)
    tower = lax.all_to_all(copies, "gz", 0, 0, tiled=True)
    return (moved(tower, "gx", -1), tower, moved(tower, "gx", 1)), beside


def slope_column(values):
    count = lax.axis_size("gx") * lax.axis_size("gz")
    copies = jnp.broadcast_to(values[None], (count,) + values.shape)
    plane = lax.all_to_all(copies, ("gx", "gz"), 0, 0, tiled=True)
    (column,) = call(pick_kernel, [shaped(12, 8, 128)], [VMEM])(plane)
    return column


def per_device(positions, velocities, forces, counts, pair_tiles, pair_count, mig_slots):
    live_count = counts.reshape(1)
    total = pair_count.reshape(1)
    steps = mig_slots.shape[0]
    slots = mig_slots.reshape(steps, 4, 128)
    atoms = shaped(3, 8, 128)
    block = shaped(8, 128)
    columns = shaped(32, 128, 128)
    slope_columns = shaped(8, 128, 128)
    atoms_scratch = pltpu.VMEM((3, 8, 128), jnp.float32)
    plan_shape = jax.ShapeDtypeStruct((8, 128), jnp.int32)

    def pair_scratch(comps, sums, *found):
        return (
            pltpu.SMEM((8, 128), jnp.int32),
            pltpu.VMEM((37, comps, 8, 128), jnp.float32),
            pltpu.VMEM((8 * sums, 128, 128), jnp.float32),
            *found,
            pltpu.SemaphoreType.DMA,
        )

    rows = jnp.concatenate([a.reshape(3, 8, 128) for a in (positions, velocities, forces)], axis=0)
    place, speed, slots, *packed = call(
        pack_kernel,
        [atoms, atoms, jax.ShapeDtypeStruct(slots.shape, jnp.int32)] + [block] * 4,
        [VMEM] * 2,
    )(rows, slots)
    plans = call(
        plan_kernel, [plan_shape, plan_shape, block], [SMEM, SMEM, VMEM]
    )(total, live_count, pair_tiles.reshape(2, 128))
    for n in range(steps):
        place, speed, sent = call(
            functools.partial(unpack_kernel, n), [atoms, atoms, atoms], [SMEM] + [VMEM] * 7
        )(live_count, place, speed, slots, *migrants(packed))
        cells, plans = around(sent, plans)
        density_plan, force_plan, selves = plans
        column, early = call(
            early_density_kernel,
            [columns, block],
            [ANY, VMEM],
            pair_scratch(3, 1),
            mega_ops=60,
        )(density_plan, cells[1])
        (slope,) = call(
            late_density_kernel,
            [block],
            [ANY] + [VMEM] * 6,
            pair_scratch(3, 1, pltpu.VMEM((8, 128), jnp.float32)),
        )(density_plan, selves, early, column, *cells)
        here = slope_column(slope)
        below, above = moved(here, "gy", -1), moved(here, "gy", 1)
        slopes, early = call(
            early_force_kernel,
            [slope_columns, atoms],
            [ANY] + [VMEM] * 6,
            pair_scratch(4, 3),
            mega_ops=60,
        )(force_plan, *cells, column, slope, here)
        last = n + 1 == steps
        place, speed, *packed = call(
            functools.partial(late_force_kernel, None if last else n + 1),
            [atoms, atoms] + [block] * (0 if last else 4),
            [ANY] + [VMEM] * (10 if last else 11),
            pair_scratch(4, 3, atoms_scratch),
        )(
            force_plan,
            *cells,
            column,
            below,
            above,
            slopes,
            early,
            place,
            speed,
            *(() if last else (slots,)),
        )
    return (place.reshape(positions.shape), speed.reshape(velocities.shape))


def solution(mesh):
    placed = (
        P(None, "gx", "gy", "gz", None),
        P(None, "gx", "gy", "gz", None),
        P(None, "gx", "gy", "gz", None),
        P("gx", "gy", "gz"),
        P(None, "gx", "gy", "gz", None),
        P("gx", "gy", "gz"),
        P(None, None, "gx", "gy", "gz", None),
    )
    return jax.shard_map(
        per_device,
        mesh=mesh,
        in_specs=placed,
        out_specs=(P(None, "gx", "gy", "gz", None), P(None, "gx", "gy", "gz", None)),
        check_vma=False,
    )
```

```python
import functools

import jax
import jax.numpy as jnp
from jax import lax
from jax.experimental import pallas as pl
from jax.experimental.pallas import tpu as pltpu
from jax.sharding import PartitionSpec as P

cutoff_sq = 0.81
cutoff = 0.9
height_ratio = 0.25
density_scale = 1.0 / 256.0
repulsion = 1.0 / 512.0
time_step = 0.25
kick = 0.5 * time_step
flat_scale = 1.0 / cutoff
tall_scale = height_ratio / cutoff
cube_factor = -8.0 * repulsion / cutoff_sq
slope_factor = -6.0 * density_scale / cutoff_sq
far_away = 1e15

VMEM = pl.BlockSpec(memory_space=pltpu.VMEM)
ANY = pl.BlockSpec(memory_space=pl.ANY)
SMEM = pl.BlockSpec(memory_space=pltpu.SMEM)
unrolled = 4
nt_dims = (((1,), (1,)), ((), ()))
nn_dims = (((1,), (0,)), ((), ()))


def dot(left, right, dims):
    return lax.dot_general(left, right, dims, preferred_element_type=jnp.float32)


def pieces(values, count):
    out = []
    for _ in range(count):
        part = values.astype(jnp.bfloat16)
        out.append(part)
        values = values - part.astype(jnp.float32)
    return out


def parity(axis):
    return lax.axis_index(axis) & 1


def away(kind, axis):
    return (2 - 2 * parity(axis), 1, 2 * parity(axis))[kind]


swaps = (("gy", 2), ("gx", 2), ("gy", 0), ("gx", 0))


def slot_masks(slots_ref, axis, kind):
    row = (0 if axis == "gx" else 2) + 1 - away(kind, axis) // 2
    slots = slots_ref[pl.ds(row, 1), :]
    lane_hit = lax.broadcasted_iota(jnp.int32, (128, 128), 0) == (slots & 127)
    tile_hit = lax.broadcasted_iota(jnp.int32, (8, 128), 0) == (slots >> 7)
    return jnp.where(lane_hit, 1.0, 0.0).astype(jnp.bfloat16), tile_hit


def drift_and_pack(place, speed, push, slots_ref, place_ref, speed_ref, packed_refs):
    speed = [speed[c] + kick * push[c] for c in range(3)]
    rates = (time_step, time_step, time_step / height_ratio)
    place = [place[c] + rates[c] * speed[c] for c in range(3)]
    for c in range(3):
        place_ref[c] = place[c]
        speed_ref[c] = speed[c]
    rows = jnp.concatenate(place + speed, axis=0)
    split = jnp.concatenate(pieces(rows, 3), axis=0)
    for (axis, kind), packed_ref in zip(swaps, packed_refs):
        lane_hit, tile_hit = slot_masks(slots_ref, axis, kind)
        found = dot(split, lane_hit, nn_dims)
        found = found[0:48] + found[48:96] + found[96:144]
        for c in range(6):
            chosen = jnp.where(tile_hit, found[8 * c : 8 * c + 8], 0.0)
            packed_ref[c : c + 1, :] = jnp.sum(chosen, axis=0, keepdims=True)
        packed_ref[6:8, :] = jnp.zeros((2, 128), jnp.float32)


def put_plan(listed, near, far, late, plan_ref):
    lanes = lax.broadcasted_iota(jnp.int32, (1, 128), 1)
    part = jnp.where(listed, jnp.where(late, near + 8, near), -1)
    rows = lax.broadcasted_iota(jnp.int32, (16, 128), 0)
    mine = jnp.where(rows == part, 1.0, 0.0).astype(jnp.bfloat16)
    before = lax.broadcasted_iota(jnp.int32, (128, 128), 0) < lax.broadcasted_iota(
        jnp.int32, (128, 128), 1
    )
    rank = dot(mine, jnp.where(before, 1.0, 0.0).astype(jnp.bfloat16), nn_dims)
    count = dot(mine, jnp.ones((128, 128), jnp.bfloat16), nn_dims)
    groups = (count.astype(jnp.int32) + (unrolled - 1)) // unrolled
    place = jnp.full((1, 128), -1, jnp.int32)
    start = jnp.zeros((1, 128), jnp.int32)
    starts = jnp.zeros((1, 128), jnp.int32)
    for t in range(16):
        at = start * unrolled + rank[t : t + 1].astype(jnp.int32)
        place = jnp.where(part == t, at, place)
        starts = jnp.where(lanes == t, start, starts)
        start = start + groups[t : t + 1]
    starts = jnp.where(lanes == 16, start, starts)
    values = jnp.where(
        rows == 0,
        (far >> 3).astype(jnp.float32),
        jnp.where(rows == 1, (far & 7).astype(jnp.float32), 1.0),
    ).astype(jnp.bfloat16)
    for half in range(2):
        spot = lax.broadcasted_iota(jnp.int32, (128, 128), 0) + 128 * half
        sent = jnp.where(spot == place, 1.0, 0.0).astype(jnp.bfloat16)
        sorted_rows = dot(values, sent, nt_dims).astype(jnp.int32)
        brick = jnp.where(sorted_rows[2:3] > 0, sorted_rows[0:1], 36)
        plan_ref[half : half + 1, :] = brick * 8 + sorted_rows[1:2]
    plan_ref[2:3, :] = starts
    plan_ref[3:8, :] = jnp.zeros((5, 128), jnp.int32)


def plan_kernel(total_ref, count_ref, tiles_ref, density_plan, force_plan, selves_ref):
    zbrick = lax.axis_index("gz")
    near = tiles_ref[0:1, :]
    far = tiles_ref[1:2, :]
    listed = lax.broadcasted_iota(jnp.int32, (1, 128), 1) < total_ref[0]
    listed = jnp.logical_and(listed, near * 128 < count_ref[0])
    brick = far >> 3
    put_plan(listed, near, far, jnp.logical_or(brick < 12, brick >= 24), density_plan)
    put_plan(listed, near, far, ((brick >> 2) + 2) % 3 != 0, force_plan)
    rows = lax.broadcasted_iota(jnp.int32, (16, 128), 0)
    itself = jnp.logical_and(listed, far == (16 + zbrick) * 8 + near)
    itself = jnp.where(jnp.logical_and(itself, rows == near), 1.0, 0.0).astype(jnp.bfloat16)
    selves_ref[...] = dot(itself, jnp.ones((128, 128), jnp.bfloat16), nn_dims)[0:8]


def pack_kernel(rows_in, place_ref, speed_ref, slots_out, *packed_refs):
    steps = slots_out.shape[0]
    for n in range(steps):
        slots_out[n] = rows_in[9, 4 * n : 4 * n + 4].astype(jnp.int32)
    drift_and_pack(
        [rows_in[c] for c in range(3)],
        [rows_in[c + 3] for c in range(3)],
        [rows_in[c + 6] for c in range(3)],
        slots_out.at[0],
        place_ref,
        speed_ref,
        packed_refs,
    )


def unpack_kernel(
    step, count_ref, place_in, speed_in, slots_in, a0, a1, a2, a3, place_ref, speed_ref, sent_ref
):
    slots_ref = slots_in.at[step]
    total = jnp.zeros((160, 128), jnp.float32)
    for (axis, kind), arrived in zip(swaps, (a0, a1, a2, a3)):
        lane_hit, tile_hit = slot_masks(slots_ref, axis, kind)
        component = 0 if axis == "gx" else 1
        shift = (away(kind, axis) - 1).astype(jnp.float32)
        rows = []
        for c in range(6):
            row = arrived[c : c + 1, :]
            if c == component:
                row = row + shift
            rows.append(jnp.where(tile_hit, row, 0.0))
        marks = jnp.where(tile_hit, 1.0, 0.0)
        split = pieces(jnp.concatenate(rows, axis=0), 3)
        split.append(jnp.concatenate([marks, jnp.zeros_like(marks)], axis=0).astype(jnp.bfloat16))
        total = total + dot(jnp.concatenate(split, axis=0), lane_hit, nt_dims)
    put = total[0:48] + total[48:96] + total[96:144]
    taken = total[144:152] > 0.5
    slot_ids = lax.broadcasted_iota(jnp.int32, (8, 128), 0) * 128 + lax.broadcasted_iota(
        jnp.int32, (8, 128), 1
    )
    live = slot_ids < count_ref[0]
    scales = (flat_scale, flat_scale, tall_scale)
    for c in range(3):
        place = jnp.where(taken, put[8 * c : 8 * c + 8], place_in[c])
        place_ref[c] = place
        speed_ref[c] = jnp.where(taken, put[24 + 8 * c : 32 + 8 * c], speed_in[c])
        sent_ref[c] = jnp.where(live, place * scales[c], far_away)


def put_ghosts(cells, ghost_ref, wanted):
    zbrick = lax.axis_index("gz")
    for kind_x, cell in enumerate(cells):
        dx = away(kind_x, "gx")
        for kind_y in range(3):
            if not wanted(kind_x, kind_y):
                continue
            dy = away(kind_y, "gy")
            for level in range(4):
                brick = dx * 12 + dy * 4 + level
                shifts = (
                    (jnp.float32(dx) - 1.5) * flat_scale,
                    (jnp.float32(dy) - 1.5) * flat_scale,
                    ((level - zbrick).astype(jnp.float32) - 0.5) * tall_scale,
                )
                for c in range(3):
                    ghost_ref[brick, c] = cell[level, kind_y, c] + shifts[c]
    ghost_ref[36] = jnp.full(ghost_ref.shape[1:], far_away, jnp.float32)


def own_places(middle):
    zbrick = lax.axis_index("gz")
    own = [middle[zbrick, 1, c] for c in range(3)]
    live = own[0] < 0.5 * far_away
    shifts = (0.5 * flat_scale, 0.5 * flat_scale, 0.5 * tall_scale)
    return [jnp.where(live, row - shift, -far_away) for row, shift in zip(own, shifts)], live


def put_columns(rows, column_ref):
    turned = jnp.concatenate(rows, axis=0).T
    for at in range(8 * len(rows)):
        column_ref[at] = jnp.broadcast_to(turned[:, at : at + 1], (128, 128))


def row_sums(block):
    first = block.astype(jnp.bfloat16)
    second = (block - first.astype(jnp.float32)).astype(jnp.bfloat16)
    split = jnp.concatenate([first, second], axis=1)
    sums = dot(split, jnp.ones((256, 128), jnp.bfloat16), nn_dims)
    on_line = lax.broadcasted_iota(jnp.int32, (128, 128), 0) == lax.broadcasted_iota(
        jnp.int32, (128, 128), 1
    )
    return jnp.sum(jnp.where(on_line, sums, 0.0), axis=0, keepdims=True)


def over_entries(plan_in, plan_ref, sem, late, prepare, body):
    copy = pltpu.make_async_copy(plan_in, plan_ref, sem)
    copy.start()
    prepare()
    copy.wait()

    def over_tile(near, carry):
        def over_group(group, carry):
            first = group * unrolled
            codes = [plan_ref[(first + i) >> 7, (first + i) & 127] for i in range(unrolled)]
            body(near, [(code >> 3, code & 7) for code in codes])
            return carry

        segment = near + 8 * late
        return lax.fori_loop(plan_ref[2, segment], plan_ref[2, segment + 1], over_group, carry)

    lax.fori_loop(0, 8, over_tile, 0)


def density_sums(plan_in, cells, column_ref, late, plan_ref, ghost_ref, sum_ref, sem):
    def prepare():
        put_ghosts(cells, ghost_ref, lambda kind_x, kind_y: (kind_x != 1) == late)
        sum_ref[...] = jnp.zeros_like(sum_ref)

    def add(near, ghosts):
        far = []
        for brick, tile in ghosts:
            x, y, z = (ghost_ref[brick, c, pl.ds(tile, 1), :] for c in range(3))
            rows = (2.0 * x, 2.0 * y, 2.0 * z, 0.5 - (x * x + y * y + z * z))
            far.append([jnp.broadcast_to(row, (8, 128)) for row in rows])
        for r in range(16):
            part = pl.ds(8 * r, 8)
            ax, ay, az, rest = (column_ref[8 * c + near, part, :] for c in range(4))
            total = sum_ref[near, part, :]
            for cx, cy, cz, cn in far:
                shrink = jnp.maximum((ax * cx + ay * cy) + (az * cz + (rest + cn)), 0.0)
                total = total + shrink * shrink * shrink
            sum_ref[near, part, :] = total

    over_entries(plan_in, plan_ref, sem, late, prepare, add)


def early_density_kernel(
    plan_in, middle, column_ref, early_ref, plan_ref, ghost_ref, sum_ref, sem
):
    own, _ = own_places(middle)
    rest = 0.5 - (own[0] * own[0] + own[1] * own[1] + own[2] * own[2])
    put_columns(own + [rest], column_ref)
    cells = (None, middle, None)
    density_sums(plan_in, cells, column_ref, False, plan_ref, ghost_ref, sum_ref, sem)
    for t in range(8):
        early_ref[t : t + 1, :] = row_sums(sum_ref[t])


def late_density_kernel(
    plan_in,
    selves_ref,
    early_ref,
    column_ref,
    beside,
    middle,
    beyond,
    slope_ref,
    plan_ref,
    ghost_ref,
    sum_ref,
    row_ref,
    sem,
):
    cells = (beside, middle, beyond)
    density_sums(plan_in, cells, column_ref, True, plan_ref, ghost_ref, sum_ref, sem)
    for t in range(8):
        row_ref[t : t + 1, :] = row_sums(sum_ref[t])
    _, live = own_places(middle)
    itself = jnp.where(live, selves_ref[...], 0.0)
    density = (row_ref[...] + early_ref[...] - itself) * density_scale
    slope_ref[...] = (-0.5 * slope_factor / cube_factor) / jnp.sqrt(1.0 + density)


def force_sums(
    plan_in, cells, slope_cells, column_ref, slopes_ref, late, plan_ref, ghost_ref, sum_ref, sem
):
    def prepare():
        put_ghosts(cells, ghost_ref, lambda kind_x, kind_y: (kind_y != 1) == late)
        for kind, cell in enumerate(slope_cells):
            if (kind != 1) == late:
                dy = away(kind, "gy")
                for dx in range(3):
                    for level in range(4):
                        ghost_ref[dx * 12 + dy * 4 + level, 3] = cell[dx * 4 + level]
        sum_ref[...] = jnp.zeros_like(sum_ref)

    def add(near, ghosts):
        far = []
        for brick, tile in ghosts:
            rows = [ghost_ref[brick, c, pl.ds(tile, 1), :] for c in range(4)]
            far.append([jnp.broadcast_to(row, (8, 128)) for row in rows])
        for r in range(16):
            part = pl.ds(8 * r, 8)
            ax, ay, az = (column_ref[8 * c + near, part, :] for c in range(3))
            slope = slopes_ref[near, part, :]
            sums = [sum_ref[8 * c + near, part, :] for c in range(3)]
            for cx, cy, cz, far_slope in far:
                dx = ax - cx
                dy = ay - cy
                dz = az - cz
                shrink = jnp.maximum(1.0 - (dx * dx + dy * dy + dz * dz), 0.0)
                weight = shrink * shrink * (shrink + (slope + far_slope))
                sums = [sums[0] + weight * dx, sums[1] + weight * dy, sums[2] + weight * dz]
            for c in range(3):
                sum_ref[8 * c + near, part, :] = sums[c]

    over_entries(plan_in, plan_ref, sem, late, prepare, add)


def early_force_kernel(
    plan_in,
    c0,
    c1,
    c2,
    column_ref,
    own_slope,
    s1,
    slopes_ref,
    early_ref,
    plan_ref,
    ghost_ref,
    sum_ref,
    sem,
):
    put_columns([own_slope[...]], slopes_ref)
    force_sums(
        plan_in,
        (c0, c1, c2),
        (None, s1, None),
        column_ref,
        slopes_ref,
        False,
        plan_ref,
        ghost_ref,
        sum_ref,
        sem,
    )
    for c in range(3):
        for t in range(8):
            early_ref[c, t : t + 1, :] = row_sums(sum_ref[8 * c + t])


def late_force_kernel(
    step,
    plan_in,
    c0,
    c1,
    c2,
    column_ref,
    s0,
    s2,
    slopes_ref,
    early_ref,
    place_in,
    speed_in,
    *rest,
):
    *outs, plan_ref, ghost_ref, sum_ref, push_ref, sem = rest
    force_sums(
        plan_in,
        (c0, c1, c2),
        (s0, None, s2),
        column_ref,
        slopes_ref,
        True,
        plan_ref,
        ghost_ref,
        sum_ref,
        sem,
    )
    for c in range(3):
        for t in range(8):
            push_ref[c, t : t + 1, :] = row_sums(sum_ref[8 * c + t])
    push = [(-cutoff * cube_factor) * (push_ref[c] + early_ref[c]) for c in range(3)]
    place = [place_in[c] for c in range(3)]
    speed = [speed_in[c] + kick * push[c] for c in range(3)]
    if step is None:
        place_ref, speed_ref = outs
        for c in range(3):
            place_ref[c] = place[c]
            speed_ref[c] = speed[c]
    else:
        slots_ref, place_ref, speed_ref, *packed = outs
        drift_and_pack(place, speed, push, slots_ref.at[step], place_ref, speed_ref, packed)


def pick_kernel(plane_ref, column_ref):
    count = lax.axis_size("gx")
    xbrick = lax.axis_index("gx")
    for dx in range(3):
        at = lax.rem(xbrick + (dx - 1 + count), count)
        for level in range(4):
            column_ref[dx * 4 + level] = plane_ref[at * 4 + level]


def shaped(*extent):
    return jax.ShapeDtypeStruct(extent, jnp.float32)


def call(kernel, outs, specs, scratch=(), mega_ops=1):
    return pl.pallas_call(
        kernel,
        out_shape=outs,
        in_specs=specs,
        out_specs=[VMEM] * len(outs),
        scratch_shapes=list(scratch),
        compiler_params=pltpu.CompilerParams(vmem_limit_bytes=24 * 2**20),
        cost_estimate=pl.CostEstimate(
            flops=mega_ops * 10**6, bytes_accessed=mega_ops * 10**5, transcendentals=0
        ),
    )


def swapped(values, axis, kind):
    count = lax.axis_size(axis)
    shift = 0 if kind == 0 else 1
    other = [((i + shift) % count ^ 1) - shift for i in range(count)]
    return lax.ppermute(values, axis, [(i, other[i] % count) for i in range(count)])


def around(values, beside):
    ends, beside = lax.optimization_barrier(
        ((swapped(values, "gy", 0), swapped(values, "gy", 2)), beside)
    )
    rows = jnp.stack([ends[0], values, ends[1]])
    copies = jnp.broadcast_to(rows[None], (4,) + rows.shape)
    tower = lax.all_to_all(copies, "gz", 0, 0, tiled=True)
    return (swapped(tower, "gx", 0), tower, swapped(tower, "gx", 2)), beside


def slope_column(values):
    count = lax.axis_size("gx") * lax.axis_size("gz")
    copies = jnp.broadcast_to(values[None], (count,) + values.shape)
    plane = lax.all_to_all(copies, ("gx", "gz"), 0, 0, tiled=True)
    (column,) = call(pick_kernel, [shaped(12, 8, 128)], [VMEM])(plane)
    return column


def per_device(positions, velocities, forces, counts, pair_tiles, pair_count, mig_slots):
    live_count = counts.reshape(1)
    total = pair_count.reshape(1)
    steps = mig_slots.shape[0]
    atoms = shaped(3, 8, 128)
    block = shaped(8, 128)
    columns = shaped(32, 128, 128)
    slope_columns = shaped(8, 128, 128)
    atoms_scratch = pltpu.VMEM((3, 8, 128), jnp.float32)
    plan_shape = jax.ShapeDtypeStruct((8, 128), jnp.int32)

    def pair_scratch(comps, sums, *found):
        return (
            pltpu.SMEM((8, 128), jnp.int32),
            pltpu.VMEM((37, comps, 8, 128), jnp.float32),
            pltpu.VMEM((8 * sums, 128, 128), jnp.float32),
            *found,
            pltpu.SemaphoreType.DMA,
        )

    slots = mig_slots.reshape(1, 4 * steps, 128).astype(jnp.float32)
    slots = jnp.pad(slots, ((0, 0), (0, 8 - 4 * steps), (0, 0)))
    rows = [a.reshape(3, 8, 128) for a in (positions, velocities, forces)]
    place, speed, slots, *packed = call(
        pack_kernel,
        [atoms, atoms, jax.ShapeDtypeStruct((steps, 4, 128), jnp.int32)] + [block] * 4,
        [VMEM],
    )(jnp.concatenate(rows + [slots], axis=0))
    plans = call(
        plan_kernel, [plan_shape, plan_shape, block], [SMEM, SMEM, VMEM]
    )(total, live_count, pair_tiles.reshape(2, 128))
    for n in range(steps):
        arrived = [swapped(sent, *swap) for sent, swap in zip(packed, swaps)]
        place, speed, sent = call(
            functools.partial(unpack_kernel, n), [atoms, atoms, atoms], [SMEM] + [VMEM] * 7
        )(live_count, place, speed, slots, *arrived)
        cells, plans = around(sent, plans)
        density_plan, force_plan, selves = plans
        column, early = call(
            early_density_kernel,
            [columns, block],
            [ANY, VMEM],
            pair_scratch(3, 1),
            mega_ops=60,
        )(density_plan, cells[1])
        (slope,) = call(
            late_density_kernel,
            [block],
            [ANY] + [VMEM] * 6,
            pair_scratch(3, 1, pltpu.VMEM((8, 128), jnp.float32)),
        )(density_plan, selves, early, column, *cells)
        here = slope_column(slope)
        ends = swapped(here, "gy", 0), swapped(here, "gy", 2)
        slopes, early = call(
            early_force_kernel,
            [slope_columns, atoms],
            [ANY] + [VMEM] * 6,
            pair_scratch(4, 3),
            mega_ops=60,
        )(force_plan, *cells, column, slope, here)
        last = n + 1 == steps
        place, speed, *packed = call(
            functools.partial(late_force_kernel, None if last else n + 1),
            [atoms, atoms] + [block] * (0 if last else 4),
            [ANY] + [VMEM] * (10 if last else 11),
            pair_scratch(4, 3, atoms_scratch),
        )(
            force_plan,
            *cells,
            column,
            *ends,
            slopes,
            early,
            place,
            speed,
            *(() if last else (slots,)),
        )
    return (place.reshape(positions.shape), speed.reshape(velocities.shape))


def solution(mesh):
    placed = (
        P(None, "gx", "gy", "gz", None),
        P(None, "gx", "gy", "gz", None),
        P(None, "gx", "gy", "gz", None),
        P("gx", "gy", "gz"),
        P(None, "gx", "gy", "gz", None),
        P("gx", "gy", "gz"),
        P(None, None, "gx", "gy", "gz", None),
    )
    return jax.shard_map(
        per_device,
        mesh=mesh,
        in_specs=placed,
        out_specs=(P(None, "gx", "gy", "gz", None), P(None, "gx", "gy", "gz", None)),
        check_vma=False,
    )
```

```python
import functools

import jax
import jax.numpy as jnp
from jax import lax
from jax.experimental import pallas as pl
from jax.experimental.pallas import tpu as pltpu
from jax.sharding import PartitionSpec as P

cutoff_sq = 0.81
cutoff = 0.9
height_ratio = 0.25
density_scale = 1.0 / 256.0
repulsion = 1.0 / 512.0
time_step = 0.25
kick = 0.5 * time_step
flat_scale = 1.0 / cutoff
tall_scale = height_ratio / cutoff
cube_factor = -8.0 * repulsion / cutoff_sq
slope_factor = -6.0 * density_scale / cutoff_sq
far_away = 1e15

VMEM = pl.BlockSpec(memory_space=pltpu.VMEM)
ANY = pl.BlockSpec(memory_space=pl.ANY)
SMEM = pl.BlockSpec(memory_space=pltpu.SMEM)
unrolled = 4
nt_dims = (((1,), (1,)), ((), ()))
nn_dims = (((1,), (0,)), ((), ()))


def dot(left, right, dims):
    return lax.dot_general(left, right, dims, preferred_element_type=jnp.float32)


def pieces(values, count):
    out = []
    for _ in range(count):
        part = values.astype(jnp.bfloat16)
        out.append(part)
        values = values - part.astype(jnp.float32)
    return out


def slot_masks(slots_ref, direction):
    slots = slots_ref[direction : direction + 1, :]
    lane_hit = lax.broadcasted_iota(jnp.int32, (128, 128), 0) == (slots & 127)
    tile_hit = lax.broadcasted_iota(jnp.int32, (8, 128), 0) == (slots >> 7)
    return jnp.where(lane_hit, 1.0, 0.0).astype(jnp.bfloat16), tile_hit


def drift_and_pack(place, speed, push, slots_ref, place_ref, speed_ref, packed_refs):
    speed = [speed[c] + kick * push[c] for c in range(3)]
    rates = (time_step, time_step, time_step / height_ratio)
    place = [place[c] + rates[c] * speed[c] for c in range(3)]
    for c in range(3):
        place_ref[c] = place[c]
        speed_ref[c] = speed[c]
    rows = jnp.concatenate(place + speed, axis=0)
    split = jnp.concatenate(pieces(rows, 3), axis=0)
    for direction in range(4):
        lane_hit, tile_hit = slot_masks(slots_ref, direction)
        found = dot(split, lane_hit, nn_dims)
        found = found[0:48] + found[48:96] + found[96:144]
        for c in range(6):
            chosen = jnp.where(tile_hit, found[8 * c : 8 * c + 8], 0.0)
            packed_refs[direction][c : c + 1, :] = jnp.sum(chosen, axis=0, keepdims=True)
        packed_refs[direction][6:8, :] = jnp.zeros((2, 128), jnp.float32)


def put_plan(listed, near, far, late, plan_ref):
    lanes = lax.broadcasted_iota(jnp.int32, (1, 128), 1)
    part = jnp.where(listed, jnp.where(late, near + 8, near), -1)
    rows = lax.broadcasted_iota(jnp.int32, (16, 128), 0)
    mine = jnp.where(rows == part, 1.0, 0.0).astype(jnp.bfloat16)
    before = lax.broadcasted_iota(jnp.int32, (128, 128), 0) < lax.broadcasted_iota(
        jnp.int32, (128, 128), 1
    )
    rank = dot(mine, jnp.where(before, 1.0, 0.0).astype(jnp.bfloat16), nn_dims)
    count = dot(mine, jnp.ones((128, 128), jnp.bfloat16), nn_dims)
    groups = (count.astype(jnp.int32) + (unrolled - 1)) // unrolled
    place = jnp.full((1, 128), -1, jnp.int32)
    start = jnp.zeros((1, 128), jnp.int32)
    starts = jnp.zeros((1, 128), jnp.int32)
    for t in range(16):
        at = start * unrolled + rank[t : t + 1].astype(jnp.int32)
        place = jnp.where(part == t, at, place)
        starts = jnp.where(lanes == t, start, starts)
        start = start + groups[t : t + 1]
    starts = jnp.where(lanes == 16, start, starts)
    values = jnp.where(
        rows == 0,
        (far >> 3).astype(jnp.float32),
        jnp.where(rows == 1, (far & 7).astype(jnp.float32), 1.0),
    ).astype(jnp.bfloat16)
    for half in range(2):
        spot = lax.broadcasted_iota(jnp.int32, (128, 128), 0) + 128 * half
        sent = jnp.where(spot == place, 1.0, 0.0).astype(jnp.bfloat16)
        sorted_rows = dot(values, sent, nt_dims).astype(jnp.int32)
        brick = jnp.where(sorted_rows[2:3] > 0, sorted_rows[0:1], 36)
        plan_ref[half : half + 1, :] = brick * 8 + sorted_rows[1:2]
    plan_ref[2:3, :] = starts
    plan_ref[3:8, :] = jnp.zeros((5, 128), jnp.int32)


def plan_kernel(total_ref, count_ref, tiles_ref, plan_ref, selves_ref):
    zbrick = lax.axis_index("gz")
    near = tiles_ref[0:1, :]
    far = tiles_ref[1:2, :]
    listed = lax.broadcasted_iota(jnp.int32, (1, 128), 1) < total_ref[0]
    listed = jnp.logical_and(listed, near * 128 < count_ref[0])
    put_plan(listed, near, far, ((far >> 5) + 2) % 3 != 0, plan_ref)
    rows = lax.broadcasted_iota(jnp.int32, (16, 128), 0)
    itself = jnp.logical_and(listed, far == (16 + zbrick) * 8 + near)
    itself = jnp.where(jnp.logical_and(itself, rows == near), 1.0, 0.0).astype(jnp.bfloat16)
    selves_ref[...] = dot(itself, jnp.ones((128, 128), jnp.bfloat16), nn_dims)[0:8]


def pack_kernel(rows_in, slots_in, place_ref, speed_ref, slots_out, *packed_refs):
    slots_out[...] = slots_in[...]
    drift_and_pack(
        [rows_in[c] for c in range(3)],
        [rows_in[c + 3] for c in range(3)],
        [rows_in[c + 6] for c in range(3)],
        slots_in.at[0],
        place_ref,
        speed_ref,
        packed_refs,
    )


def unpack_kernel(
    step, count_ref, place_in, speed_in, slots_in, a0, a1, a2, a3, place_ref, speed_ref, sent_ref
):
    slots_ref = slots_in.at[step]
    total = jnp.zeros((160, 128), jnp.float32)
    plan = ((a0, 0, 1.0), (a1, 0, -1.0), (a2, 1, 1.0), (a3, 1, -1.0))
    for direction, (arrived, component, shift) in enumerate(plan):
        lane_hit, tile_hit = slot_masks(slots_ref, direction)
        rows = []
        for c in range(6):
            row = arrived[c : c + 1, :]
            if c == component:
                row = row + shift
            rows.append(jnp.where(tile_hit, row, 0.0))
        marks = jnp.where(tile_hit, 1.0, 0.0)
        split = pieces(jnp.concatenate(rows, axis=0), 3)
        split.append(jnp.concatenate([marks, jnp.zeros_like(marks)], axis=0).astype(jnp.bfloat16))
        total = total + dot(jnp.concatenate(split, axis=0), lane_hit, nt_dims)
    put = total[0:48] + total[48:96] + total[96:144]
    taken = total[144:152] > 0.5
    slot_ids = lax.broadcasted_iota(jnp.int32, (8, 128), 0) * 128 + lax.broadcasted_iota(
        jnp.int32, (8, 128), 1
    )
    live = slot_ids < count_ref[0]
    scales = (flat_scale, flat_scale, tall_scale)
    for c in range(3):
        place = jnp.where(taken, put[8 * c : 8 * c + 8], place_in[c])
        place_ref[c] = place
        speed_ref[c] = jnp.where(taken, put[24 + 8 * c : 32 + 8 * c], speed_in[c])
        sent_ref[c] = jnp.where(live, place * scales[c], far_away)


def put_ghosts(cells, ghost_ref, late):
    zbrick = lax.axis_index("gz")
    for dy, cell in enumerate(cells):
        if (dy != 1) != late:
            continue
        for dx in range(3):
            for level in range(4):
                rise = ((level - zbrick).astype(jnp.float32) - 0.5) * tall_scale
                brick = dx * 12 + dy * 4 + level
                ghost_ref[brick, 0] = cell[dx * 4 + level, 0] + (dx - 1.5) * flat_scale
                ghost_ref[brick, 1] = cell[dx * 4 + level, 1] + (dy - 1.5) * flat_scale
                ghost_ref[brick, 2] = cell[dx * 4 + level, 2] + rise
    ghost_ref[36] = jnp.full(ghost_ref.shape[1:], far_away, jnp.float32)


def own_places(here):
    at = lax.axis_index("gz") + 4
    own = [here[at, c] for c in range(3)]
    live = own[0] < 0.5 * far_away
    shifts = (0.5 * flat_scale, 0.5 * flat_scale, 0.5 * tall_scale)
    return [jnp.where(live, row - shift, -far_away) for row, shift in zip(own, shifts)], live


def put_columns(rows, column_ref):
    turned = jnp.concatenate(rows, axis=0).T
    for at in range(8 * len(rows)):
        column_ref[at] = jnp.broadcast_to(turned[:, at : at + 1], (128, 128))


def row_sums(block):
    first = block.astype(jnp.bfloat16)
    second = (block - first.astype(jnp.float32)).astype(jnp.bfloat16)
    split = jnp.concatenate([first, second], axis=1)
    sums = dot(split, jnp.ones((256, 128), jnp.bfloat16), nn_dims)
    on_line = lax.broadcasted_iota(jnp.int32, (128, 128), 0) == lax.broadcasted_iota(
        jnp.int32, (128, 128), 1
    )
    return jnp.sum(jnp.where(on_line, sums, 0.0), axis=0, keepdims=True)


def over_entries(plan_in, plan_ref, sem, late, prepare, body):
    copy = pltpu.make_async_copy(plan_in, plan_ref, sem)
    copy.start()
    prepare()
    copy.wait()
    begin = plan_ref[2, 8] if late else 0

    def over_tile(near, carry):
        def over_group(group, carry):
            first = group * unrolled
            codes = [plan_ref[(first + i) >> 7, (first + i) & 127] for i in range(unrolled)]
            spots = [(group - begin) * unrolled + i for i in range(unrolled)]
            body(near, [(code >> 3, code & 7) for code in codes], spots)
            return carry

        segment = near + 8 * late
        return lax.fori_loop(plan_ref[2, segment], plan_ref[2, segment + 1], over_group, carry)

    lax.fori_loop(0, 8, over_tile, 0)


def density_sums(plan_in, cells, column_ref, late, shrink_ref, plan_ref, ghost_ref, sum_ref, sem):
    def prepare():
        put_ghosts(cells, ghost_ref, late)
        sum_ref[...] = jnp.zeros_like(sum_ref)

    def add(near, ghosts, spots):
        far = []
        for brick, tile in ghosts:
            x, y, z = (ghost_ref[brick, c, pl.ds(tile, 1), :] for c in range(3))
            rows = (2.0 * x, 2.0 * y, 2.0 * z, 0.5 - (x * x + y * y + z * z))
            far.append([jnp.broadcast_to(row, (8, 128)) for row in rows])
        for r in range(16):
            part = pl.ds(8 * r, 8)
            ax, ay, az, rest = (column_ref[8 * c + near, part, :] for c in range(4))
            total = sum_ref[near, part, :]
            for (cx, cy, cz, cn), spot in zip(far, spots):
                shrink = jnp.maximum((ax * cx + ay * cy) + (az * cz + (rest + cn)), 0.0)
                shrink_ref[spot, part, :] = shrink
                total = total + shrink * shrink * shrink
            sum_ref[near, part, :] = total

    over_entries(plan_in, plan_ref, sem, late, prepare, add)


def early_density_kernel(
    plan_in, here, column_ref, early_ref, shrink_ref, plan_ref, ghost_ref, sum_ref, sem
):
    own, _ = own_places(here)
    rest = 0.5 - (own[0] * own[0] + own[1] * own[1] + own[2] * own[2])
    put_columns(own + [rest], column_ref)
    cells = (None, here, None)
    density_sums(plan_in, cells, column_ref, False, shrink_ref, plan_ref, ghost_ref, sum_ref, sem)
    for t in range(8):
        early_ref[t : t + 1, :] = row_sums(sum_ref[t])


def late_density_kernel(
    plan_in,
    selves_ref,
    early_ref,
    column_ref,
    below,
    here,
    above,
    slope_ref,
    shrink_ref,
    plan_ref,
    ghost_ref,
    sum_ref,
    row_ref,
    sem,
):
    cells = (below, here, above)
    density_sums(plan_in, cells, column_ref, True, shrink_ref, plan_ref, ghost_ref, sum_ref, sem)
    for t in range(8):
        row_ref[t : t + 1, :] = row_sums(sum_ref[t])
    _, live = own_places(here)
    itself = jnp.where(live, selves_ref[...], 0.0)
    density = (row_ref[...] + early_ref[...] - itself) * density_scale
    slope_ref[0] = (-0.5 * slope_factor / cube_factor) / jnp.sqrt(1.0 + density)


def force_sums(
    plan_in,
    cells,
    slope_cells,
    column_ref,
    slopes_ref,
    shrink_ref,
    late,
    plan_ref,
    ghost_ref,
    sum_ref,
    sem,
):
    def prepare():
        put_ghosts(cells, ghost_ref, late)
        for dy, cell in enumerate(slope_cells):
            if (dy != 1) == late:
                for dx in range(3):
                    for level in range(4):
                        ghost_ref[dx * 12 + dy * 4 + level, 3] = cell[dx * 4 + level, 0]
        sum_ref[...] = jnp.zeros_like(sum_ref)

    def add(near, ghosts, spots):
        far = []
        for brick, tile in ghosts:
            rows = [ghost_ref[brick, c, pl.ds(tile, 1), :] for c in range(4)]
            far.append([jnp.broadcast_to(row, (8, 128)) for row in rows])
        for r in range(16):
            part = pl.ds(8 * r, 8)
            place = [column_ref[8 * c + near, part, :] for c in range(3)]
            slope = slopes_ref[near, part, :]
            sums = [sum_ref[8 * c + near, part, :] for c in range(3)]
            for rows, spot in zip(far, spots):
                shrink = shrink_ref[spot, part, :]
                weight = shrink * shrink * (shrink + (slope + rows[3]))
                sums = [sums[c] + weight * (place[c] - rows[c]) for c in range(3)]
            for c in range(3):
                sum_ref[8 * c + near, part, :] = sums[c]

    over_entries(plan_in, plan_ref, sem, late, prepare, add)


def early_force_kernel(
    plan_in,
    here,
    column_ref,
    own_slope,
    slope_here,
    shrink_ref,
    slopes_ref,
    early_ref,
    plan_ref,
    ghost_ref,
    sum_ref,
    sem,
):
    put_columns([own_slope[0]], slopes_ref)
    force_sums(
        plan_in,
        (None, here, None),
        (None, slope_here, None),
        column_ref,
        slopes_ref,
        shrink_ref,
        False,
        plan_ref,
        ghost_ref,
        sum_ref,
        sem,
    )
    for c in range(3):
        for t in range(8):
            early_ref[c, t : t + 1, :] = row_sums(sum_ref[8 * c + t])


def late_force_kernel(
    step,
    plan_in,
    below,
    above,
    column_ref,
    slope_below,
    slope_above,
    shrink_ref,
    slopes_ref,
    early_ref,
    place_in,
    speed_in,
    *rest,
):
    *outs, plan_ref, ghost_ref, sum_ref, push_ref, sem = rest
    force_sums(
        plan_in,
        (below, None, above),
        (slope_below, None, slope_above),
        column_ref,
        slopes_ref,
        shrink_ref,
        True,
        plan_ref,
        ghost_ref,
        sum_ref,
        sem,
    )
    for c in range(3):
        for t in range(8):
            push_ref[c, t : t + 1, :] = row_sums(sum_ref[8 * c + t])
    push = [(-cutoff * cube_factor) * (push_ref[c] + early_ref[c]) for c in range(3)]
    place = [place_in[c] for c in range(3)]
    speed = [speed_in[c] + kick * push[c] for c in range(3)]
    if step is None:
        place_ref, speed_ref = outs
        for c in range(3):
            place_ref[c] = place[c]
            speed_ref[c] = speed[c]
    else:
        slots_ref, place_ref, speed_ref, *packed = outs
        drift_and_pack(place, speed, push, slots_ref.at[step], place_ref, speed_ref, packed)


def pick_kernel(plane_ref, column_ref):
    count = lax.axis_size("gx")
    xbrick = lax.axis_index("gx")
    for dx in range(3):
        at = lax.rem(xbrick + (dx - 1 + count), count)
        for level in range(4):
            column_ref[dx * 4 + level] = plane_ref[at * 4 + level]


def shaped(*extent):
    return jax.ShapeDtypeStruct(extent, jnp.float32)


def call(kernel, outs, specs, scratch=(), mega_ops=1):
    return pl.pallas_call(
        kernel,
        out_shape=outs,
        in_specs=specs,
        out_specs=[VMEM] * len(outs),
        scratch_shapes=list(scratch),
        compiler_params=pltpu.CompilerParams(vmem_limit_bytes=24 * 2**20),
        cost_estimate=pl.CostEstimate(
            flops=mega_ops * 10**6, bytes_accessed=mega_ops * 10**5, transcendentals=0
        ),
    )


def moved(values, axis, shift):
    count = lax.axis_size(axis)
    return lax.ppermute(values, axis, [((i + shift) % count, i) for i in range(count)])


def migrants(packed):
    return (
        moved(packed[1], "gx", 1),
        moved(packed[0], "gx", -1),
        moved(packed[3], "gy", 1),
        moved(packed[2], "gy", -1),
    )


def row_around(values):
    count = lax.axis_size("gx") * lax.axis_size("gz")
    copies = jnp.broadcast_to(values[None], (count,) + values.shape)
    plane = lax.all_to_all(copies, ("gx", "gz"), 0, 0, tiled=True)
    (row,) = call(pick_kernel, [shaped(12, *values.shape)], [VMEM])(plane)
    return row


def beside(row):
    return moved(row, "gy", -1), moved(row, "gy", 1)


def per_device(positions, velocities, forces, counts, pair_tiles, pair_count, mig_slots):
    live_count = counts.reshape(1)
    total = pair_count.reshape(1)
    steps = mig_slots.shape[0]
    slots = mig_slots.reshape(steps, 4, 128)
    atoms = shaped(3, 8, 128)
    block = shaped(8, 128)
    slope_block = shaped(1, 8, 128)
    columns = shaped(32, 128, 128)
    shrinks = shaped(128 + 8 * (unrolled - 1), 128, 128)
    slope_columns = shaped(8, 128, 128)
    atoms_scratch = pltpu.VMEM((3, 8, 128), jnp.float32)
    plan_shape = jax.ShapeDtypeStruct((8, 128), jnp.int32)

    def pair_scratch(comps, sums, *found):
        return (
            pltpu.SMEM((8, 128), jnp.int32),
            pltpu.VMEM((37, comps, 8, 128), jnp.float32),
            pltpu.VMEM((8 * sums, 128, 128), jnp.float32),
            *found,
            pltpu.SemaphoreType.DMA,
        )

    rows = jnp.concatenate([a.reshape(3, 8, 128) for a in (positions, velocities, forces)], axis=0)
    place, speed, slots, *packed = call(
        pack_kernel,
        [atoms, atoms, jax.ShapeDtypeStruct(slots.shape, jnp.int32)] + [block] * 4,
        [VMEM] * 2,
    )(rows, slots)
    plan, selves = call(plan_kernel, [plan_shape, block], [SMEM, SMEM, VMEM])(
        total, live_count, pair_tiles.reshape(2, 128)
    )
    for n in range(steps):
        arrived, (plan, selves) = lax.optimization_barrier((migrants(packed), (plan, selves)))
        place, speed, sent = call(
            functools.partial(unpack_kernel, n), [atoms, atoms, atoms], [SMEM] + [VMEM] * 7
        )(live_count, place, speed, slots, *arrived)
        here = row_around(sent)
        below, above = beside(here)
        column, early, early_shrinks = call(
            early_density_kernel,
            [columns, block, shrinks],
            [ANY, VMEM],
            pair_scratch(3, 1),
            mega_ops=60,
        )(plan, here)
        slope, late_shrinks = call(
            late_density_kernel,
            [slope_block, shrinks],
            [ANY] + [VMEM] * 6,
            pair_scratch(3, 1, pltpu.VMEM((8, 128), jnp.float32)),
        )(plan, selves, early, column, below, here, above)
        slope_here = row_around(slope)
        slope_below, slope_above = beside(slope_here)
        slopes, early = call(
            early_force_kernel,
            [slope_columns, atoms],
            [ANY] + [VMEM] * 5,
            pair_scratch(4, 3),
            mega_ops=60,
        )(plan, here, column, slope, slope_here, early_shrinks)
        last = n + 1 == steps
        place, speed, *packed = call(
            functools.partial(late_force_kernel, None if last else n + 1),
            [atoms, atoms] + [block] * (0 if last else 4),
            [ANY] + [VMEM] * (10 if last else 11),
            pair_scratch(4, 3, atoms_scratch),
        )(
            plan,
            below,
            above,
            column,
            slope_below,
            slope_above,
            late_shrinks,
            slopes,
            early,
            place,
            speed,
            *(() if last else (slots,)),
        )
    return (place.reshape(positions.shape), speed.reshape(velocities.shape))


def solution(mesh):
    placed = (
        P(None, "gx", "gy", "gz", None),
        P(None, "gx", "gy", "gz", None),
        P(None, "gx", "gy", "gz", None),
        P("gx", "gy", "gz"),
        P(None, "gx", "gy", "gz", None),
        P("gx", "gy", "gz"),
        P(None, None, "gx", "gy", "gz", None),
    )
    return jax.shard_map(
        per_device,
        mesh=mesh,
        in_specs=placed,
        out_specs=(P(None, "gx", "gy", "gz", None), P(None, "gx", "gy", "gz", None)),
        check_vma=False,
    )
```

```python
import functools

import jax
import jax.numpy as jnp
from jax import lax
from jax.experimental import pallas as pl
from jax.experimental.pallas import tpu as pltpu
from jax.sharding import PartitionSpec as P

cutoff_sq = 0.81
cutoff = 0.9
height_ratio = 0.25
density_scale = 1.0 / 256.0
repulsion = 1.0 / 512.0
time_step = 0.25
kick = 0.5 * time_step
flat_scale = 1.0 / cutoff
tall_scale = height_ratio / cutoff
cube_factor = -8.0 * repulsion / cutoff_sq
slope_factor = -6.0 * density_scale / cutoff_sq
far_away = 1e15

VMEM = pl.BlockSpec(memory_space=pltpu.VMEM)
ANY = pl.BlockSpec(memory_space=pl.ANY)
SMEM = pl.BlockSpec(memory_space=pltpu.SMEM)
unrolled = 4
nothing = 128
unused = 129
nt_dims = (((1,), (1,)), ((), ()))
nn_dims = (((1,), (0,)), ((), ()))


def dot(left, right, dims):
    return lax.dot_general(left, right, dims, preferred_element_type=jnp.float32)


def pieces(values, count):
    out = []
    for _ in range(count):
        part = values.astype(jnp.bfloat16)
        out.append(part)
        values = values - part.astype(jnp.float32)
    return out


def slot_masks(slots_ref, direction):
    slots = slots_ref[direction : direction + 1, :]
    lane_hit = lax.broadcasted_iota(jnp.int32, (128, 128), 0) == (slots & 127)
    tile_hit = lax.broadcasted_iota(jnp.int32, (8, 128), 0) == (slots >> 7)
    return jnp.where(lane_hit, 1.0, 0.0).astype(jnp.bfloat16), tile_hit


def drift_and_pack(place, speed, push, slots_ref, place_ref, speed_ref, packed_refs):
    speed = [speed[c] + kick * push[c] for c in range(3)]
    rates = (time_step, time_step, time_step / height_ratio)
    place = [place[c] + rates[c] * speed[c] for c in range(3)]
    for c in range(3):
        place_ref[c] = place[c]
        speed_ref[c] = speed[c]
    rows = jnp.concatenate(place + speed, axis=0)
    split = jnp.concatenate(pieces(rows, 3), axis=0)
    for direction in range(4):
        lane_hit, tile_hit = slot_masks(slots_ref, direction)
        found = dot(split, lane_hit, nn_dims)
        found = found[0:48] + found[48:96] + found[96:144]
        for c in range(6):
            chosen = jnp.where(tile_hit, found[8 * c : 8 * c + 8], 0.0)
            packed_refs[direction][c : c + 1, :] = jnp.sum(chosen, axis=0, keepdims=True)
        packed_refs[direction][6:8, :] = jnp.zeros((2, 128), jnp.float32)


def put_plan(listed, near, far, late, spots, empty, plan_ref):
    lanes = lax.broadcasted_iota(jnp.int32, (1, 128), 1)
    part = jnp.where(listed, jnp.where(late, near + 8, near), -1)
    rows = lax.broadcasted_iota(jnp.int32, (16, 128), 0)
    mine = jnp.where(rows == part, 1.0, 0.0).astype(jnp.bfloat16)
    before = lax.broadcasted_iota(jnp.int32, (128, 128), 0) < lax.broadcasted_iota(
        jnp.int32, (128, 128), 1
    )
    rank = dot(mine, jnp.where(before, 1.0, 0.0).astype(jnp.bfloat16), nn_dims)
    count = dot(mine, jnp.ones((128, 128), jnp.bfloat16), nn_dims)
    groups = (count.astype(jnp.int32) + (unrolled - 1)) // unrolled
    place = jnp.full((1, 128), -1, jnp.int32)
    start = jnp.zeros((1, 128), jnp.int32)
    starts = jnp.zeros((1, 128), jnp.int32)
    for t in range(16):
        at = start * unrolled + rank[t : t + 1].astype(jnp.int32)
        place = jnp.where(part == t, at, place)
        starts = jnp.where(lanes == t, start, starts)
        start = start + groups[t : t + 1]
    starts = jnp.where(lanes == 16, start, starts)
    values = jnp.where(rows == 2, 1.0, 0.0)
    for at, row in enumerate((far >> 3, far & 7, None, *spots)):
        if row is not None:
            values = jnp.where(rows == at, row.astype(jnp.float32), values)
    values = values.astype(jnp.bfloat16)
    plan_ref[7:8, :] = jnp.zeros((1, 128), jnp.int32)
    for half in range(2):
        spot = lax.broadcasted_iota(jnp.int32, (128, 128), 0) + 128 * half
        sent = jnp.where(spot == place, 1.0, 0.0).astype(jnp.bfloat16)
        sorted_rows = dot(values, sent, nt_dims).astype(jnp.int32)
        found = sorted_rows[2:3] > 0
        brick = jnp.where(found, sorted_rows[0:1], 36)
        plan_ref[half : half + 1, :] = brick * 8 + sorted_rows[1:2]
        plan_ref[3 + half : 4 + half, :] = jnp.where(found, sorted_rows[3:4], empty)
        plan_ref[5 + half : 6 + half, :] = jnp.where(found, sorted_rows[4:5], empty)
    plan_ref[2:3, :] = starts


def plan_kernel(total_ref, count_ref, tiles_ref, density_plan, force_plan, selves_ref):
    zbrick = lax.axis_index("gz")
    near = tiles_ref[0:1, :]
    far = tiles_ref[1:2, :]
    listed = lax.broadcasted_iota(jnp.int32, (1, 128), 1) < total_ref[0]
    listed = jnp.logical_and(listed, near * 128 < count_ref[0])
    brick = far >> 3
    late = jnp.logical_or(brick < 12, brick >= 24)
    spots = lax.broadcasted_iota(jnp.int32, (1, 128), 1)
    put_plan(listed, near, far, late, (spots, spots), unused, density_plan)
    spots = jnp.where(late, nothing, spots), jnp.where(late, spots, nothing)
    put_plan(listed, near, far, ((brick >> 2) + 2) % 3 != 0, spots, nothing, force_plan)
    rows = lax.broadcasted_iota(jnp.int32, (16, 128), 0)
    itself = jnp.logical_and(listed, far == (16 + zbrick) * 8 + near)
    itself = jnp.where(jnp.logical_and(itself, rows == near), 1.0, 0.0).astype(jnp.bfloat16)
    selves_ref[...] = dot(itself, jnp.ones((128, 128), jnp.bfloat16), nn_dims)[0:8]


def pack_kernel(rows_in, slots_in, place_ref, speed_ref, slots_out, *packed_refs):
    slots_out[...] = slots_in[...]
    drift_and_pack(
        [rows_in[c] for c in range(3)],
        [rows_in[c + 3] for c in range(3)],
        [rows_in[c + 6] for c in range(3)],
        slots_in.at[0],
        place_ref,
        speed_ref,
        packed_refs,
    )


def unpack_kernel(
    step, count_ref, place_in, speed_in, slots_in, a0, a1, a2, a3, place_ref, speed_ref, sent_ref
):
    slots_ref = slots_in.at[step]
    total = jnp.zeros((160, 128), jnp.float32)
    plan = ((a0, 0, 1.0), (a1, 0, -1.0), (a2, 1, 1.0), (a3, 1, -1.0))
    for direction, (arrived, component, shift) in enumerate(plan):
        lane_hit, tile_hit = slot_masks(slots_ref, direction)
        rows = []
        for c in range(6):
            row = arrived[c : c + 1, :]
            if c == component:
                row = row + shift
            rows.append(jnp.where(tile_hit, row, 0.0))
        marks = jnp.where(tile_hit, 1.0, 0.0)
        split = pieces(jnp.concatenate(rows, axis=0), 3)
        split.append(jnp.concatenate([marks, jnp.zeros_like(marks)], axis=0).astype(jnp.bfloat16))
        total = total + dot(jnp.concatenate(split, axis=0), lane_hit, nt_dims)
    put = total[0:48] + total[48:96] + total[96:144]
    taken = total[144:152] > 0.5
    slot_ids = lax.broadcasted_iota(jnp.int32, (8, 128), 0) * 128 + lax.broadcasted_iota(
        jnp.int32, (8, 128), 1
    )
    live = slot_ids < count_ref[0]
    scales = (flat_scale, flat_scale, tall_scale)
    for c in range(3):
        place = jnp.where(taken, put[8 * c : 8 * c + 8], place_in[c])
        place_ref[c] = place
        speed_ref[c] = jnp.where(taken, put[24 + 8 * c : 32 + 8 * c], speed_in[c])
        sent_ref[c] = jnp.where(live, place * scales[c], far_away)


def put_ghosts(cells, ghost_ref, wanted):
    zbrick = lax.axis_index("gz")
    for level in range(4):
        rise = ((level - zbrick).astype(jnp.float32) - 0.5) * tall_scale
        for dx, cell in enumerate(cells):
            for dy in range(3):
                if not wanted(dx, dy):
                    continue
                brick = dx * 12 + dy * 4 + level
                ghost_ref[brick, 0] = cell[level, dy, 0] + (dx - 1.5) * flat_scale
                ghost_ref[brick, 1] = cell[level, dy, 1] + (dy - 1.5) * flat_scale
                ghost_ref[brick, 2] = cell[level, dy, 2] + rise
    ghost_ref[36] = jnp.full(ghost_ref.shape[1:], far_away, jnp.float32)


def own_places(middle):
    zbrick = lax.axis_index("gz")
    own = [middle[zbrick, 1, c] for c in range(3)]
    live = own[0] < 0.5 * far_away
    shifts = (0.5 * flat_scale, 0.5 * flat_scale, 0.5 * tall_scale)
    return [jnp.where(live, row - shift, -far_away) for row, shift in zip(own, shifts)], live


def put_columns(rows, column_ref):
    turned = jnp.concatenate(rows, axis=0).T
    for at in range(8 * len(rows)):
        column_ref[at] = jnp.broadcast_to(turned[:, at : at + 1], (128, 128))


def row_sums(block):
    first = block.astype(jnp.bfloat16)
    second = (block - first.astype(jnp.float32)).astype(jnp.bfloat16)
    split = jnp.concatenate([first, second], axis=1)
    sums = dot(split, jnp.ones((256, 128), jnp.bfloat16), nn_dims)
    on_line = lax.broadcasted_iota(jnp.int32, (128, 128), 0) == lax.broadcasted_iota(
        jnp.int32, (128, 128), 1
    )
    return jnp.sum(jnp.where(on_line, sums, 0.0), axis=0, keepdims=True)


def over_entries(plan_in, plan_ref, sem, late, prepare, body):
    copy = pltpu.make_async_copy(plan_in, plan_ref, sem)
    copy.start()
    prepare()
    copy.wait()

    def over_tile(near, carry):
        def over_group(group, carry):
            places = [group * unrolled + i for i in range(unrolled)]
            places = [(place >> 7, place & 127) for place in places]
            codes = [plan_ref[row, lane] for row, lane in places]
            body(near, [(code >> 3, code & 7) for code in codes], places)
            return carry

        segment = near + 8 * late
        return lax.fori_loop(plan_ref[2, segment], plan_ref[2, segment + 1], over_group, carry)

    lax.fori_loop(0, 8, over_tile, 0)


def density_sums(plan_in, cells, column_ref, late, shrink_ref, plan_ref, ghost_ref, sum_ref, sem):
    def prepare():
        put_ghosts(cells, ghost_ref, lambda dx, dy: (dx != 1) == late)
        sum_ref[...] = jnp.zeros_like(sum_ref)
        shrink_ref[nothing] = jnp.zeros((128, 128), jnp.float32)

    def add(near, ghosts, places):
        far = []
        for (brick, tile), (row, lane) in zip(ghosts, places):
            x, y, z = (ghost_ref[brick, c, pl.ds(tile, 1), :] for c in range(3))
            rows = (2.0 * x, 2.0 * y, 2.0 * z, 0.5 - (x * x + y * y + z * z))
            rows = [jnp.broadcast_to(row, (8, 128)) for row in rows]
            far.append((rows, plan_ref[3 + row, lane]))
        for r in range(16):
            part = pl.ds(8 * r, 8)
            ax, ay, az, rest = (column_ref[8 * c + near, part, :] for c in range(4))
            total = sum_ref[near, part, :]
            for (cx, cy, cz, cn), spot in far:
                shrink = jnp.maximum((ax * cx + ay * cy) + (az * cz + (rest + cn)), 0.0)
                shrink_ref[spot, part, :] = shrink
                total = total + shrink * shrink * shrink
            sum_ref[near, part, :] = total

    over_entries(plan_in, plan_ref, sem, late, prepare, add)


def early_density_kernel(
    plan_in, middle, column_ref, early_ref, shrink_ref, plan_ref, ghost_ref, sum_ref, sem
):
    own, _ = own_places(middle)
    rest = 0.5 - (own[0] * own[0] + own[1] * own[1] + own[2] * own[2])
    put_columns(own + [rest], column_ref)
    cells = (None, middle, None)
    density_sums(plan_in, cells, column_ref, False, shrink_ref, plan_ref, ghost_ref, sum_ref, sem)
    for t in range(8):
        early_ref[t : t + 1, :] = row_sums(sum_ref[t])


def late_density_kernel(
    plan_in,
    selves_ref,
    early_ref,
    column_ref,
    behind,
    middle,
    ahead,
    slope_ref,
    shrink_ref,
    plan_ref,
    ghost_ref,
    sum_ref,
    row_ref,
    sem,
):
    cells = (behind, middle, ahead)
    density_sums(plan_in, cells, column_ref, True, shrink_ref, plan_ref, ghost_ref, sum_ref, sem)
    for t in range(8):
        row_ref[t : t + 1, :] = row_sums(sum_ref[t])
    _, live = own_places(middle)
    itself = jnp.where(live, selves_ref[...], 0.0)
    density = (row_ref[...] + early_ref[...] - itself) * density_scale
    slope_ref[...] = (-0.5 * slope_factor / cube_factor) / jnp.sqrt(1.0 + density)


def force_sums(
    plan_in,
    cells,
    slope_cells,
    column_ref,
    slopes_ref,
    shrink_refs,
    late,
    plan_ref,
    ghost_ref,
    sum_ref,
    sem,
):
    first_ref, second_ref = shrink_refs

    def prepare():
        put_ghosts(cells, ghost_ref, lambda dx, dy: (dy != 1) == late)
        for dy, cell in enumerate(slope_cells):
            if (dy != 1) == late:
                for dx in range(3):
                    for level in range(4):
                        ghost_ref[dx * 12 + dy * 4 + level, 3] = cell[dx * 4 + level]
        sum_ref[...] = jnp.zeros_like(sum_ref)

    def add(near, ghosts, places):
        far = []
        for (brick, tile), (row, lane) in zip(ghosts, places):
            rows = [ghost_ref[brick, c, pl.ds(tile, 1), :] for c in range(4)]
            rows = [jnp.broadcast_to(row, (8, 128)) for row in rows]
            far.append((rows, plan_ref[3 + row, lane], plan_ref[5 + row, lane]))
        for r in range(16):
            part = pl.ds(8 * r, 8)
            place = [column_ref[8 * c + near, part, :] for c in range(3)]
            slope = slopes_ref[near, part, :]
            sums = [sum_ref[8 * c + near, part, :] for c in range(3)]
            for rows, first, second in far:
                shrink = first_ref[first, part, :] + second_ref[second, part, :]
                weight = shrink * shrink * (shrink + (slope + rows[3]))
                sums = [sums[c] + weight * (place[c] - rows[c]) for c in range(3)]
            for c in range(3):
                sum_ref[8 * c + near, part, :] = sums[c]

    over_entries(plan_in, plan_ref, sem, late, prepare, add)


def early_force_kernel(
    plan_in,
    c0,
    c1,
    c2,
    column_ref,
    own_slope,
    s1,
    h0,
    h1,
    slopes_ref,
    early_ref,
    plan_ref,
    ghost_ref,
    sum_ref,
    sem,
):
    put_columns([own_slope[...]], slopes_ref)
    force_sums(
        plan_in,
        (c0, c1, c2),
        (None, s1, None),
        column_ref,
        slopes_ref,
        (h0, h1),
        False,
        plan_ref,
        ghost_ref,
        sum_ref,
        sem,
    )
    for c in range(3):
        for t in range(8):
            early_ref[c, t : t + 1, :] = row_sums(sum_ref[8 * c + t])


def late_force_kernel(
    step,
    plan_in,
    c0,
    c1,
    c2,
    column_ref,
    s0,
    s2,
    h0,
    h1,
    slopes_ref,
    early_ref,
    place_in,
    speed_in,
    *rest,
):
    *outs, plan_ref, ghost_ref, sum_ref, push_ref, sem = rest
    force_sums(
        plan_in,
        (c0, c1, c2),
        (s0, None, s2),
        column_ref,
        slopes_ref,
        (h0, h1),
        True,
        plan_ref,
        ghost_ref,
        sum_ref,
        sem,
    )
    for c in range(3):
        for t in range(8):
            push_ref[c, t : t + 1, :] = row_sums(sum_ref[8 * c + t])
    push = [(-cutoff * cube_factor) * (push_ref[c] + early_ref[c]) for c in range(3)]
    place = [place_in[c] for c in range(3)]
    speed = [speed_in[c] + kick * push[c] for c in range(3)]
    if step is None:
        place_ref, speed_ref = outs
        for c in range(3):
            place_ref[c] = place[c]
            speed_ref[c] = speed[c]
    else:
        slots_ref, place_ref, speed_ref, *packed = outs
        drift_and_pack(place, speed, push, slots_ref.at[step], place_ref, speed_ref, packed)


def pick_kernel(plane_ref, column_ref):
    count = lax.axis_size("gx")
    xbrick = lax.axis_index("gx")
    for dx in range(3):
        at = lax.rem(xbrick + (dx - 1 + count), count)
        for level in range(4):
            column_ref[dx * 4 + level] = plane_ref[at * 4 + level]


def shaped(*extent):
    return jax.ShapeDtypeStruct(extent, jnp.float32)


def call(kernel, outs, specs, scratch=(), mega_ops=1):
    return pl.pallas_call(
        kernel,
        out_shape=outs,
        in_specs=specs,
        out_specs=[VMEM] * len(outs),
        scratch_shapes=list(scratch),
        compiler_params=pltpu.CompilerParams(vmem_limit_bytes=24 * 2**20),
        cost_estimate=pl.CostEstimate(
            flops=mega_ops * 10**6, bytes_accessed=mega_ops * 10**5, transcendentals=0
        ),
    )


def moved(values, axis, shift):
    count = lax.axis_size(axis)
    return lax.ppermute(values, axis, [((i + shift) % count, i) for i in range(count)])


def migrants(packed):
    return (
        moved(packed[1], "gx", 1),
        moved(packed[0], "gx", -1),
        moved(packed[3], "gy", 1),
        moved(packed[2], "gy", -1),
    )


def around(values):
    rows = jnp.stack([moved(values, "gy", -1), values, moved(values, "gy", 1)])
    copies = jnp.broadcast_to(rows[None], (4,) + rows.shape)
    tower = lax.all_to_all(copies, "gz", 0, 0, tiled=True)
    return moved(tower, "gx", -1), tower, moved(tower, "gx", 1)


def slope_column(values):
    count = lax.axis_size("gx") * lax.axis_size("gz")
    copies = jnp.broadcast_to(values[None], (count,) + values.shape)
    plane = lax.all_to_all(copies, ("gx", "gz"), 0, 0, tiled=True)
    (column,) = call(pick_kernel, [shaped(12, 8, 128)], [VMEM])(plane)
    return column


def per_device(positions, velocities, forces, counts, pair_tiles, pair_count, mig_slots):
    live_count = counts.reshape(1)
    total = pair_count.reshape(1)
    steps = mig_slots.shape[0]
    slots = mig_slots.reshape(steps, 4, 128)
    atoms = shaped(3, 8, 128)
    block = shaped(8, 128)
    columns = shaped(32, 128, 128)
    slope_columns = shaped(8, 128, 128)
    atoms_scratch = pltpu.VMEM((3, 8, 128), jnp.float32)
    shrinks = shaped(130, 128, 128)
    plan_shape = jax.ShapeDtypeStruct((8, 128), jnp.int32)

    def pair_scratch(comps, sums, *found):
        return (
            pltpu.SMEM((8, 128), jnp.int32),
            pltpu.VMEM((37, comps, 8, 128), jnp.float32),
            pltpu.VMEM((8 * sums, 128, 128), jnp.float32),
            *found,
            pltpu.SemaphoreType.DMA,
        )

    rows = jnp.concatenate([a.reshape(3, 8, 128) for a in (positions, velocities, forces)], axis=0)
    place, speed, slots, *packed = call(
        pack_kernel,
        [atoms, atoms, jax.ShapeDtypeStruct(slots.shape, jnp.int32)] + [block] * 4,
        [VMEM] * 2,
    )(rows, slots)
    plans = call(
        plan_kernel, [plan_shape, plan_shape, block], [SMEM, SMEM, VMEM]
    )(total, live_count, pair_tiles.reshape(2, 128))
    for n in range(steps):
        arrived, plans = lax.optimization_barrier((migrants(packed), plans))
        density_plan, force_plan, selves = plans
        place, speed, sent = call(
            functools.partial(unpack_kernel, n), [atoms, atoms, atoms], [SMEM] + [VMEM] * 7
        )(live_count, place, speed, slots, *arrived)
        cells = around(sent)
        column, early, early_shrinks = call(
            early_density_kernel,
            [columns, block, shrinks],
            [ANY, VMEM],
            pair_scratch(3, 1),
            mega_ops=60,
        )(density_plan, cells[1])
        slope, late_shrinks = call(
            late_density_kernel,
            [block, shrinks],
            [ANY] + [VMEM] * 6,
            pair_scratch(3, 1, pltpu.VMEM((8, 128), jnp.float32)),
        )(density_plan, selves, early, column, *cells)
        here = slope_column(slope)
        below, above = moved(here, "gy", -1), moved(here, "gy", 1)
        slopes, early = call(
            early_force_kernel,
            [slope_columns, atoms],
            [ANY] + [VMEM] * 8,
            pair_scratch(4, 3),
            mega_ops=60,
        )(force_plan, *cells, column, slope, here, early_shrinks, late_shrinks)
        last = n + 1 == steps
        place, speed, *packed = call(
            functools.partial(late_force_kernel, None if last else n + 1),
            [atoms, atoms] + [block] * (0 if last else 4),
            [ANY] + [VMEM] * (12 if last else 13),
            pair_scratch(4, 3, atoms_scratch),
        )(
            force_plan,
            *cells,
            column,
            below,
            above,
            early_shrinks,
            late_shrinks,
            slopes,
            early,
            place,
            speed,
            *(() if last else (slots,)),
        )
    return (place.reshape(positions.shape), speed.reshape(velocities.shape))


def solution(mesh):
    placed = (
        P(None, "gx", "gy", "gz", None),
        P(None, "gx", "gy", "gz", None),
        P(None, "gx", "gy", "gz", None),
        P("gx", "gy", "gz"),
        P(None, "gx", "gy", "gz", None),
        P("gx", "gy", "gz"),
        P(None, None, "gx", "gy", "gz", None),
    )
    return jax.shard_map(
        per_device,
        mesh=mesh,
        in_specs=placed,
        out_specs=(P(None, "gx", "gy", "gz", None), P(None, "gx", "gy", "gz", None)),
        check_vma=False,
    )
```

```python
import functools

import jax
import jax.numpy as jnp
from jax import lax
from jax.experimental import pallas as pl
from jax.experimental.pallas import tpu as pltpu
from jax.sharding import PartitionSpec as P

cutoff_sq = 0.81
cutoff = 0.9
height_ratio = 0.25
density_scale = 1.0 / 256.0
repulsion = 1.0 / 512.0
time_step = 0.25
kick = 0.5 * time_step
flat_scale = 1.0 / cutoff
tall_scale = height_ratio / cutoff
cube_factor = -8.0 * repulsion / cutoff_sq
slope_factor = -6.0 * density_scale / cutoff_sq
far_away = 1e15

VMEM = pl.BlockSpec(memory_space=pltpu.VMEM)
ANY = pl.BlockSpec(memory_space=pl.ANY)
SMEM = pl.BlockSpec(memory_space=pltpu.SMEM)
unrolled = 4
nothing = 128
unused = 129
nt_dims = (((1,), (1,)), ((), ()))
nn_dims = (((1,), (0,)), ((), ()))


def dot(left, right, dims):
    return lax.dot_general(left, right, dims, preferred_element_type=jnp.float32)


def pieces(values, count):
    out = []
    for _ in range(count):
        part = values.astype(jnp.bfloat16)
        out.append(part)
        values = values - part.astype(jnp.float32)
    return out


def slot_masks(slots_ref, direction):
    slots = slots_ref[direction : direction + 1, :]
    lane_hit = lax.broadcasted_iota(jnp.int32, (128, 128), 0) == (slots & 127)
    tile_hit = lax.broadcasted_iota(jnp.int32, (8, 128), 0) == (slots >> 7)
    return jnp.where(lane_hit, 1.0, 0.0).astype(jnp.bfloat16), tile_hit


def drift_and_pack(place, speed, push, slots_ref, place_ref, speed_ref, packed_refs):
    speed = [speed[c] + kick * push[c] for c in range(3)]
    rates = (time_step, time_step, time_step / height_ratio)
    place = [place[c] + rates[c] * speed[c] for c in range(3)]
    for c in range(3):
        place_ref[c] = place[c]
        speed_ref[c] = speed[c]
    rows = jnp.concatenate(place + speed, axis=0)
    split = jnp.concatenate(pieces(rows, 3), axis=0)
    for direction in range(4):
        lane_hit, tile_hit = slot_masks(slots_ref, direction)
        found = dot(split, lane_hit, nn_dims)
        found = found[0:48] + found[48:96] + found[96:144]
        for c in range(6):
            chosen = jnp.where(tile_hit, found[8 * c : 8 * c + 8], 0.0)
            packed_refs[direction][c : c + 1, :] = jnp.sum(chosen, axis=0, keepdims=True)
        packed_refs[direction][6:8, :] = jnp.zeros((2, 128), jnp.float32)


def put_plan(listed, near, far, late, spots, empty, plan_ref):
    lanes = lax.broadcasted_iota(jnp.int32, (1, 128), 1)
    part = jnp.where(listed, jnp.where(late, near + 8, near), -1)
    rows = lax.broadcasted_iota(jnp.int32, (16, 128), 0)
    mine = jnp.where(rows == part, 1.0, 0.0).astype(jnp.bfloat16)
    before = lax.broadcasted_iota(jnp.int32, (128, 128), 0) < lax.broadcasted_iota(
        jnp.int32, (128, 128), 1
    )
    rank = dot(mine, jnp.where(before, 1.0, 0.0).astype(jnp.bfloat16), nn_dims)
    count = dot(mine, jnp.ones((128, 128), jnp.bfloat16), nn_dims)
    groups = (count.astype(jnp.int32) + (unrolled - 1)) // unrolled
    place = jnp.full((1, 128), -1, jnp.int32)
    start = jnp.zeros((1, 128), jnp.int32)
    starts = jnp.zeros((1, 128), jnp.int32)
    for t in range(16):
        at = start * unrolled + rank[t : t + 1].astype(jnp.int32)
        place = jnp.where(part == t, at, place)
        starts = jnp.where(lanes == t, start, starts)
        start = start + groups[t : t + 1]
    starts = jnp.where(lanes == 16, start, starts)
    values = jnp.where(rows == 2, 1.0, 0.0)
    for at, row in enumerate((far >> 3, far & 7, None, *spots)):
        if row is not None:
            values = jnp.where(rows == at, row.astype(jnp.float32), values)
    values = values.astype(jnp.bfloat16)
    plan_ref[7:8, :] = jnp.zeros((1, 128), jnp.int32)
    for half in range(2):
        spot = lax.broadcasted_iota(jnp.int32, (128, 128), 0) + 128 * half
        sent = jnp.where(spot == place, 1.0, 0.0).astype(jnp.bfloat16)
        sorted_rows = dot(values, sent, nt_dims).astype(jnp.int32)
        found = sorted_rows[2:3] > 0
        brick = jnp.where(found, sorted_rows[0:1], 36)
        plan_ref[half : half + 1, :] = brick * 8 + sorted_rows[1:2]
        plan_ref[3 + half : 4 + half, :] = jnp.where(found, sorted_rows[3:4], empty)
        plan_ref[5 + half : 6 + half, :] = jnp.where(found, sorted_rows[4:5], empty)
    plan_ref[2:3, :] = starts


def plan_kernel(total_ref, count_ref, tiles_ref, density_plan, force_plan, selves_ref):
    zbrick = lax.axis_index("gz")
    near = tiles_ref[0:1, :]
    far = tiles_ref[1:2, :]
    listed = lax.broadcasted_iota(jnp.int32, (1, 128), 1) < total_ref[0]
    listed = jnp.logical_and(listed, near * 128 < count_ref[0])
    brick = far >> 3
    late = jnp.logical_or(brick < 12, brick >= 24)
    spots = lax.broadcasted_iota(jnp.int32, (1, 128), 1)
    put_plan(listed, near, far, late, (spots, spots), unused, density_plan)
    spots = jnp.where(late, nothing, spots), jnp.where(late, spots, nothing)
    put_plan(listed, near, far, ((brick >> 2) + 2) % 3 != 0, spots, nothing, force_plan)
    rows = lax.broadcasted_iota(jnp.int32, (16, 128), 0)
    itself = jnp.logical_and(listed, far == (16 + zbrick) * 8 + near)
    itself = jnp.where(jnp.logical_and(itself, rows == near), 1.0, 0.0).astype(jnp.bfloat16)
    selves_ref[...] = dot(itself, jnp.ones((128, 128), jnp.bfloat16), nn_dims)[0:8]


def pack_kernel(rows_in, slots_in, place_ref, speed_ref, slots_out, *packed_refs):
    slots_out[...] = slots_in[...]
    drift_and_pack(
        [rows_in[c] for c in range(3)],
        [rows_in[c + 3] for c in range(3)],
        [rows_in[c + 6] for c in range(3)],
        slots_in.at[0],
        place_ref,
        speed_ref,
        packed_refs,
    )


def unpack_kernel(
    step, count_ref, place_in, speed_in, slots_in, a2, a3, a0, a1, place_ref, speed_ref, sent_ref
):
    slots_ref = slots_in.at[step]
    total = jnp.zeros((160, 128), jnp.float32)
    plan = ((a0, 0, 1.0), (a1, 0, -1.0), (a2, 1, 1.0), (a3, 1, -1.0))
    for direction, (arrived, component, shift) in enumerate(plan):
        lane_hit, tile_hit = slot_masks(slots_ref, direction)
        rows = []
        for c in range(6):
            row = arrived[c : c + 1, :]
            if c == component:
                row = row + shift
            rows.append(jnp.where(tile_hit, row, 0.0))
        marks = jnp.where(tile_hit, 1.0, 0.0)
        split = pieces(jnp.concatenate(rows, axis=0), 3)
        split.append(jnp.concatenate([marks, jnp.zeros_like(marks)], axis=0).astype(jnp.bfloat16))
        total = total + dot(jnp.concatenate(split, axis=0), lane_hit, nt_dims)
    put = total[0:48] + total[48:96] + total[96:144]
    taken = total[144:152] > 0.5
    slot_ids = lax.broadcasted_iota(jnp.int32, (8, 128), 0) * 128 + lax.broadcasted_iota(
        jnp.int32, (8, 128), 1
    )
    live = slot_ids < count_ref[0]
    scales = (flat_scale, flat_scale, tall_scale)
    for c in range(3):
        place = jnp.where(taken, put[8 * c : 8 * c + 8], place_in[c])
        place_ref[c] = place
        speed_ref[c] = jnp.where(taken, put[24 + 8 * c : 32 + 8 * c], speed_in[c])
        sent_ref[c] = jnp.where(live, place * scales[c], far_away)


def put_ghosts(cells, ghost_ref, wanted):
    zbrick = lax.axis_index("gz")
    for level in range(4):
        rise = ((level - zbrick).astype(jnp.float32) - 0.5) * tall_scale
        for dx, cell in enumerate(cells):
            for dy in range(3):
                if not wanted(dx, dy):
                    continue
                brick = dx * 12 + dy * 4 + level
                ghost_ref[brick, 0] = cell[level, dy, 0] + (dx - 1.5) * flat_scale
                ghost_ref[brick, 1] = cell[level, dy, 1] + (dy - 1.5) * flat_scale
                ghost_ref[brick, 2] = cell[level, dy, 2] + rise
    ghost_ref[36] = jnp.full(ghost_ref.shape[1:], far_away, jnp.float32)


def own_places(middle):
    zbrick = lax.axis_index("gz")
    own = [middle[zbrick, 1, c] for c in range(3)]
    live = own[0] < 0.5 * far_away
    shifts = (0.5 * flat_scale, 0.5 * flat_scale, 0.5 * tall_scale)
    return [jnp.where(live, row - shift, -far_away) for row, shift in zip(own, shifts)], live


def put_columns(rows, column_ref):
    turned = jnp.concatenate(rows, axis=0).T
    for at in range(8 * len(rows)):
        column_ref[at] = jnp.broadcast_to(turned[:, at : at + 1], (128, 128))


def row_sums(block):
    first = block.astype(jnp.bfloat16)
    second = (block - first.astype(jnp.float32)).astype(jnp.bfloat16)
    split = jnp.concatenate([first, second], axis=1)
    sums = dot(split, jnp.ones((256, 128), jnp.bfloat16), nn_dims)
    on_line = lax.broadcasted_iota(jnp.int32, (128, 128), 0) == lax.broadcasted_iota(
        jnp.int32, (128, 128), 1
    )
    return jnp.sum(jnp.where(on_line, sums, 0.0), axis=0, keepdims=True)


def over_entries(plan_in, plan_ref, sem, late, prepare, body):
    copy = pltpu.make_async_copy(plan_in, plan_ref, sem)
    copy.start()
    prepare()
    copy.wait()

    def over_tile(near, carry):
        def over_group(group, carry):
            places = [group * unrolled + i for i in range(unrolled)]
            places = [(place >> 7, place & 127) for place in places]
            codes = [plan_ref[row, lane] for row, lane in places]
            body(near, [(code >> 3, code & 7) for code in codes], places)
            return carry

        segment = near + 8 * late
        return lax.fori_loop(plan_ref[2, segment], plan_ref[2, segment + 1], over_group, carry)

    lax.fori_loop(0, 8, over_tile, 0)


def density_sums(plan_in, cells, column_ref, late, shrink_ref, plan_ref, ghost_ref, sum_ref, sem):
    def prepare():
        put_ghosts(cells, ghost_ref, lambda dx, dy: (dx != 1) == late)
        sum_ref[...] = jnp.zeros_like(sum_ref)
        shrink_ref[nothing] = jnp.zeros((128, 128), jnp.float32)

    def add(near, ghosts, places):
        far = []
        for (brick, tile), (row, lane) in zip(ghosts, places):
            x, y, z = (ghost_ref[brick, c, pl.ds(tile, 1), :] for c in range(3))
            rows = (2.0 * x, 2.0 * y, 2.0 * z, 0.5 - (x * x + y * y + z * z))
            rows = [jnp.broadcast_to(row, (8, 128)) for row in rows]
            far.append((rows, plan_ref[3 + row, lane]))
        for r in range(16):
            part = pl.ds(8 * r, 8)
            ax, ay, az, rest = (column_ref[8 * c + near, part, :] for c in range(4))
            total = sum_ref[near, part, :]
            for (cx, cy, cz, cn), spot in far:
                shrink = jnp.maximum((ax * cx + ay * cy) + (az * cz + (rest + cn)), 0.0)
                shrink_ref[spot, part, :] = shrink
                total = total + shrink * shrink * shrink
            sum_ref[near, part, :] = total

    over_entries(plan_in, plan_ref, sem, late, prepare, add)


def early_density_kernel(
    plan_in, middle, column_ref, early_ref, shrink_ref, plan_ref, ghost_ref, sum_ref, sem
):
    own, _ = own_places(middle)
    rest = 0.5 - (own[0] * own[0] + own[1] * own[1] + own[2] * own[2])
    put_columns(own + [rest], column_ref)
    cells = (None, middle, None)
    density_sums(plan_in, cells, column_ref, False, shrink_ref, plan_ref, ghost_ref, sum_ref, sem)
    for t in range(8):
        early_ref[t : t + 1, :] = row_sums(sum_ref[t])


def late_density_kernel(
    plan_in,
    selves_ref,
    early_ref,
    column_ref,
    behind,
    middle,
    ahead,
    slope_ref,
    shrink_ref,
    plan_ref,
    ghost_ref,
    sum_ref,
    row_ref,
    sem,
):
    cells = (behind, middle, ahead)
    density_sums(plan_in, cells, column_ref, True, shrink_ref, plan_ref, ghost_ref, sum_ref, sem)
    for t in range(8):
        row_ref[t : t + 1, :] = row_sums(sum_ref[t])
    _, live = own_places(middle)
    itself = jnp.where(live, selves_ref[...], 0.0)
    density = (row_ref[...] + early_ref[...] - itself) * density_scale
    slope_ref[...] = (-0.5 * slope_factor / cube_factor) / jnp.sqrt(1.0 + density)


def force_sums(
    plan_in,
    cells,
    slope_cells,
    column_ref,
    slopes_ref,
    shrink_refs,
    late,
    plan_ref,
    ghost_ref,
    sum_ref,
    sem,
):
    first_ref, second_ref = shrink_refs

    def prepare():
        put_ghosts(cells, ghost_ref, lambda dx, dy: (dy != 1) == late)
        for dy, cell in enumerate(slope_cells):
            if (dy != 1) == late:
                for dx in range(3):
                    for level in range(4):
                        ghost_ref[dx * 12 + dy * 4 + level, 3] = cell[dx * 4 + level]
        sum_ref[...] = jnp.zeros_like(sum_ref)

    def add(near, ghosts, places):
        far = []
        for (brick, tile), (row, lane) in zip(ghosts, places):
            rows = [ghost_ref[brick, c, pl.ds(tile, 1), :] for c in range(4)]
            rows = [jnp.broadcast_to(row, (8, 128)) for row in rows]
            far.append((rows, plan_ref[3 + row, lane], plan_ref[5 + row, lane]))
        for r in range(16):
            part = pl.ds(8 * r, 8)
            place = [column_ref[8 * c + near, part, :] for c in range(3)]
            slope = slopes_ref[near, part, :]
            sums = [sum_ref[8 * c + near, part, :] for c in range(3)]
            for rows, first, second in far:
                shrink = first_ref[first, part, :] + second_ref[second, part, :]
                weight = shrink * shrink * (shrink + (slope + rows[3]))
                sums = [sums[c] + weight * (place[c] - rows[c]) for c in range(3)]
            for c in range(3):
                sum_ref[8 * c + near, part, :] = sums[c]

    over_entries(plan_in, plan_ref, sem, late, prepare, add)


def early_force_kernel(
    plan_in,
    c0,
    c1,
    c2,
    column_ref,
    own_slope,
    s1,
    h0,
    h1,
    slopes_ref,
    early_ref,
    plan_ref,
    ghost_ref,
    sum_ref,
    sem,
):
    put_columns([own_slope[...]], slopes_ref)
    force_sums(
        plan_in,
        (c0, c1, c2),
        (None, s1, None),
        column_ref,
        slopes_ref,
        (h0, h1),
        False,
        plan_ref,
        ghost_ref,
        sum_ref,
        sem,
    )
    for c in range(3):
        for t in range(8):
            early_ref[c, t : t + 1, :] = row_sums(sum_ref[8 * c + t])


def late_force_kernel(
    step,
    plan_in,
    c0,
    c1,
    c2,
    column_ref,
    s0,
    s2,
    h0,
    h1,
    slopes_ref,
    early_ref,
    place_in,
    speed_in,
    *rest,
):
    *outs, plan_ref, ghost_ref, sum_ref, push_ref, sem = rest
    force_sums(
        plan_in,
        (c0, c1, c2),
        (s0, None, s2),
        column_ref,
        slopes_ref,
        (h0, h1),
        True,
        plan_ref,
        ghost_ref,
        sum_ref,
        sem,
    )
    for c in range(3):
        for t in range(8):
            push_ref[c, t : t + 1, :] = row_sums(sum_ref[8 * c + t])
    push = [(-cutoff * cube_factor) * (push_ref[c] + early_ref[c]) for c in range(3)]
    place = [place_in[c] for c in range(3)]
    speed = [speed_in[c] + kick * push[c] for c in range(3)]
    if step is None:
        place_ref, speed_ref = outs
        for c in range(3):
            place_ref[c] = place[c]
            speed_ref[c] = speed[c]
    else:
        slots_ref, place_ref, speed_ref, *packed = outs
        drift_and_pack(place, speed, push, slots_ref.at[step], place_ref, speed_ref, packed)


def pick_kernel(plane_ref, column_ref):
    count = lax.axis_size("gx")
    xbrick = lax.axis_index("gx")
    for dx in range(3):
        at = lax.rem(xbrick + (dx - 1 + count), count)
        for level in range(4):
            column_ref[dx * 4 + level] = plane_ref[at * 4 + level]


def shaped(*extent):
    return jax.ShapeDtypeStruct(extent, jnp.float32)


def call(kernel, outs, specs, scratch=(), mega_ops=1):
    return pl.pallas_call(
        kernel,
        out_shape=outs,
        in_specs=specs,
        out_specs=[VMEM] * len(outs),
        scratch_shapes=list(scratch),
        compiler_params=pltpu.CompilerParams(vmem_limit_bytes=24 * 2**20),
        cost_estimate=pl.CostEstimate(
            flops=mega_ops * 10**6, bytes_accessed=mega_ops * 10**5, transcendentals=0
        ),
    )


def moved(values, axis, shift):
    count = lax.axis_size(axis)
    return lax.ppermute(values, axis, [((i + shift) % count, i) for i in range(count)])


def migrants(packed):
    return (
        moved(packed[3], "gy", 1),
        moved(packed[2], "gy", -1),
        moved(packed[1], "gx", 1),
        moved(packed[0], "gx", -1),
    )


def around(values):
    rows = jnp.stack([moved(values, "gy", -1), values, moved(values, "gy", 1)])
    copies = jnp.broadcast_to(rows[None], (4,) + rows.shape)
    tower = lax.all_to_all(copies, "gz", 0, 0, tiled=True)
    return moved(tower, "gx", -1), tower, moved(tower, "gx", 1)


def slope_column(values):
    count = lax.axis_size("gx") * lax.axis_size("gz")
    copies = jnp.broadcast_to(values[None], (count,) + values.shape)
    plane = lax.all_to_all(copies, ("gx", "gz"), 0, 0, tiled=True)
    (column,) = call(pick_kernel, [shaped(12, 8, 128)], [VMEM])(plane)
    return column


def per_device(positions, velocities, forces, counts, pair_tiles, pair_count, mig_slots):
    live_count = counts.reshape(1)
    total = pair_count.reshape(1)
    steps = mig_slots.shape[0]
    slots = mig_slots.reshape(steps, 4, 128)
    atoms = shaped(3, 8, 128)
    block = shaped(8, 128)
    columns = shaped(32, 128, 128)
    slope_columns = shaped(8, 128, 128)
    atoms_scratch = pltpu.VMEM((3, 8, 128), jnp.float32)
    shrinks = shaped(130, 128, 128)
    plan_shape = jax.ShapeDtypeStruct((8, 128), jnp.int32)

    def pair_scratch(comps, sums, *found):
        return (
            pltpu.SMEM((8, 128), jnp.int32),
            pltpu.VMEM((37, comps, 8, 128), jnp.float32),
            pltpu.VMEM((8 * sums, 128, 128), jnp.float32),
            *found,
            pltpu.SemaphoreType.DMA,
        )

    rows = jnp.concatenate([a.reshape(3, 8, 128) for a in (positions, velocities, forces)], axis=0)
    place, speed, slots, *packed = call(
        pack_kernel,
        [atoms, atoms, jax.ShapeDtypeStruct(slots.shape, jnp.int32)] + [block] * 4,
        [VMEM] * 2,
    )(rows, slots)
    plans = call(
        plan_kernel, [plan_shape, plan_shape, block], [SMEM, SMEM, VMEM]
    )(total, live_count, pair_tiles.reshape(2, 128))
    for n in range(steps):
        arrived, plans = lax.optimization_barrier((migrants(packed), plans))
        density_plan, force_plan, selves = plans
        place, speed, sent = call(
            functools.partial(unpack_kernel, n), [atoms, atoms, atoms], [SMEM] + [VMEM] * 7
        )(live_count, place, speed, slots, *arrived)
        cells = around(sent)
        column, early, early_shrinks = call(
            early_density_kernel,
            [columns, block, shrinks],
            [ANY, VMEM],
            pair_scratch(3, 1),
            mega_ops=60,
        )(density_plan, cells[1])
        slope, late_shrinks = call(
            late_density_kernel,
            [block, shrinks],
            [ANY] + [VMEM] * 6,
            pair_scratch(3, 1, pltpu.VMEM((8, 128), jnp.float32)),
        )(density_plan, selves, early, column, *cells)
        here = slope_column(slope)
        below, above = moved(here, "gy", -1), moved(here, "gy", 1)
        slopes, early = call(
            early_force_kernel,
            [slope_columns, atoms],
            [ANY] + [VMEM] * 8,
            pair_scratch(4, 3),
            mega_ops=60,
        )(force_plan, *cells, column, slope, here, early_shrinks, late_shrinks)
        last = n + 1 == steps
        place, speed, *packed = call(
            functools.partial(late_force_kernel, None if last else n + 1),
            [atoms, atoms] + [block] * (0 if last else 4),
            [ANY] + [VMEM] * (12 if last else 13),
            pair_scratch(4, 3, atoms_scratch),
        )(
            force_plan,
            *cells,
            column,
            below,
            above,
            early_shrinks,
            late_shrinks,
            slopes,
            early,
            place,
            speed,
            *(() if last else (slots,)),
        )
    return (place.reshape(positions.shape), speed.reshape(velocities.shape))


def solution(mesh):
    placed = (
        P(None, "gx", "gy", "gz", None),
        P(None, "gx", "gy", "gz", None),
        P(None, "gx", "gy", "gz", None),
        P("gx", "gy", "gz"),
        P(None, "gx", "gy", "gz", None),
        P("gx", "gy", "gz"),
        P(None, None, "gx", "gy", "gz", None),
    )
    return jax.shard_map(
        per_device,
        mesh=mesh,
        in_specs=placed,
        out_specs=(P(None, "gx", "gy", "gz", None), P(None, "gx", "gy", "gz", None)),
        check_vma=False,
    )
```

```python
import functools

import jax
import jax.numpy as jnp
from jax import lax
from jax.experimental import pallas as pl
from jax.experimental.pallas import tpu as pltpu
from jax.sharding import PartitionSpec as P

cutoff_sq = 0.81
cutoff = 0.9
height_ratio = 0.25
density_scale = 1.0 / 256.0
repulsion = 1.0 / 512.0
time_step = 0.25
kick = 0.5 * time_step
flat_scale = 1.0 / cutoff
tall_scale = height_ratio / cutoff
cube_factor = -8.0 * repulsion / cutoff_sq
slope_factor = -6.0 * density_scale / cutoff_sq
far_away = 1e15

VMEM = pl.BlockSpec(memory_space=pltpu.VMEM)
ANY = pl.BlockSpec(memory_space=pl.ANY)
SMEM = pl.BlockSpec(memory_space=pltpu.SMEM)
unrolled = 4
nt_dims = (((1,), (1,)), ((), ()))
nn_dims = (((1,), (0,)), ((), ()))


def dot(left, right, dims):
    return lax.dot_general(left, right, dims, preferred_element_type=jnp.float32)


def pieces(values, count):
    out = []
    for _ in range(count):
        part = values.astype(jnp.bfloat16)
        out.append(part)
        values = values - part.astype(jnp.float32)
    return out


def slot_masks(slots_ref, direction):
    slots = slots_ref[direction : direction + 1, :]
    lane_hit = lax.broadcasted_iota(jnp.int32, (128, 128), 0) == (slots & 127)
    tile_hit = lax.broadcasted_iota(jnp.int32, (8, 128), 0) == (slots >> 7)
    return jnp.where(lane_hit, 1.0, 0.0).astype(jnp.bfloat16), tile_hit


def drift_and_pack(place, speed, push, slots_ref, place_ref, speed_ref, packed_refs):
    speed = [speed[c] + kick * push[c] for c in range(3)]
    rates = (time_step, time_step, time_step / height_ratio)
    place = [place[c] + rates[c] * speed[c] for c in range(3)]
    for c in range(3):
        place_ref[c] = place[c]
        speed_ref[c] = speed[c]
    rows = jnp.concatenate(place + speed, axis=0)
    split = jnp.concatenate(pieces(rows, 3), axis=0)
    for direction in range(4):
        lane_hit, tile_hit = slot_masks(slots_ref, direction)
        found = dot(split, lane_hit, nn_dims)
        found = found[0:48] + found[48:96] + found[96:144]
        for c in range(6):
            chosen = jnp.where(tile_hit, found[8 * c : 8 * c + 8], 0.0)
            packed_refs[direction][c : c + 1, :] = jnp.sum(chosen, axis=0, keepdims=True)
        packed_refs[direction][6:8, :] = jnp.zeros((2, 128), jnp.float32)


def put_plan(listed, near, far, late, plan_ref):
    lanes = lax.broadcasted_iota(jnp.int32, (1, 128), 1)
    part = jnp.where(listed, jnp.where(late, near + 8, near), -1)
    rows = lax.broadcasted_iota(jnp.int32, (16, 128), 0)
    mine = jnp.where(rows == part, 1.0, 0.0).astype(jnp.bfloat16)
    before = lax.broadcasted_iota(jnp.int32, (128, 128), 0) < lax.broadcasted_iota(
        jnp.int32, (128, 128), 1
    )
    rank = dot(mine, jnp.where(before, 1.0, 0.0).astype(jnp.bfloat16), nn_dims)
    count = dot(mine, jnp.ones((128, 128), jnp.bfloat16), nn_dims)
    groups = (count.astype(jnp.int32) + (unrolled - 1)) // unrolled
    place = jnp.full((1, 128), -1, jnp.int32)
    start = jnp.zeros((1, 128), jnp.int32)
    starts = jnp.zeros((1, 128), jnp.int32)
    for t in range(16):
        at = start * unrolled + rank[t : t + 1].astype(jnp.int32)
        place = jnp.where(part == t, at, place)
        starts = jnp.where(lanes == t, start, starts)
        start = start + groups[t : t + 1]
    starts = jnp.where(lanes == 16, start, starts)
    values = jnp.where(
        rows == 0,
        (far >> 3).astype(jnp.float32),
        jnp.where(rows == 1, (far & 7).astype(jnp.float32), 1.0),
    ).astype(jnp.bfloat16)
    for half in range(2):
        spot = lax.broadcasted_iota(jnp.int32, (128, 128), 0) + 128 * half
        sent = jnp.where(spot == place, 1.0, 0.0).astype(jnp.bfloat16)
        sorted_rows = dot(values, sent, nt_dims).astype(jnp.int32)
        brick = jnp.where(sorted_rows[2:3] > 0, sorted_rows[0:1], 36)
        plan_ref[half : half + 1, :] = brick * 8 + sorted_rows[1:2]
    plan_ref[2:3, :] = starts
    plan_ref[3:8, :] = jnp.zeros((5, 128), jnp.int32)


def live_ghosts(cells, far):
    lanes = lax.broadcasted_iota(jnp.int32, (8, 128), 1)
    rows = lax.broadcasted_iota(jnp.int32, (8, 128), 0)
    first = jnp.zeros((8, 128), jnp.float32)
    for dx, cell in enumerate(cells):
        for dy in range(3):
            for level in range(4):
                column = jnp.broadcast_to(cell[level, dy, 0][:, 0:1], (8, 128))
                first = jnp.where(lanes == dx * 12 + dy * 4 + level, column, first)
    live = jnp.where(first < 0.5 * far_away, 1.0, 0.0)
    live = jnp.concatenate([live, jnp.zeros_like(live)], axis=0).astype(jnp.bfloat16)
    bricks = lax.broadcasted_iota(jnp.int32, (128, 128), 0) == (far >> 3)
    found = dot(live, jnp.where(bricks, 1.0, 0.0).astype(jnp.bfloat16), nn_dims)[0:8]
    return jnp.sum(jnp.where(rows == (far & 7), found, 0.0), axis=0, keepdims=True) > 0.5


def plan_kernel(total_ref, count_ref, tiles_ref, *rest):
    *cells, density_plan, force_plan, selves_ref = rest
    zbrick = lax.axis_index("gz")
    near = tiles_ref[0:1, :]
    far = tiles_ref[1:2, :]
    listed = lax.broadcasted_iota(jnp.int32, (1, 128), 1) < total_ref[0]
    listed = jnp.logical_and(listed, near * 128 < count_ref[0])
    if cells:
        listed = jnp.logical_and(listed, live_ghosts(cells, far))
    brick = far >> 3
    put_plan(listed, near, far, jnp.logical_or(brick < 12, brick >= 24), density_plan)
    put_plan(listed, near, far, ((brick >> 2) + 2) % 3 != 0, force_plan)
    rows = lax.broadcasted_iota(jnp.int32, (16, 128), 0)
    itself = jnp.logical_and(listed, far == (16 + zbrick) * 8 + near)
    itself = jnp.where(jnp.logical_and(itself, rows == near), 1.0, 0.0).astype(jnp.bfloat16)
    selves_ref[...] = dot(itself, jnp.ones((128, 128), jnp.bfloat16), nn_dims)[0:8]


def pack_kernel(rows_in, slots_in, place_ref, speed_ref, slots_out, *packed_refs):
    slots_out[...] = slots_in[...]
    drift_and_pack(
        [rows_in[c] for c in range(3)],
        [rows_in[c + 3] for c in range(3)],
        [rows_in[c + 6] for c in range(3)],
        slots_in.at[0],
        place_ref,
        speed_ref,
        packed_refs,
    )


def unpack_kernel(
    step, count_ref, place_in, speed_in, slots_in, a0, a1, a2, a3, place_ref, speed_ref, sent_ref
):
    slots_ref = slots_in.at[step]
    total = jnp.zeros((160, 128), jnp.float32)
    plan = ((a0, 0, 1.0), (a1, 0, -1.0), (a2, 1, 1.0), (a3, 1, -1.0))
    for direction, (arrived, component, shift) in enumerate(plan):
        lane_hit, tile_hit = slot_masks(slots_ref, direction)
        rows = []
        for c in range(6):
            row = arrived[c : c + 1, :]
            if c == component:
                row = row + shift
            rows.append(jnp.where(tile_hit, row, 0.0))
        marks = jnp.where(tile_hit, 1.0, 0.0)
        split = pieces(jnp.concatenate(rows, axis=0), 3)
        split.append(jnp.concatenate([marks, jnp.zeros_like(marks)], axis=0).astype(jnp.bfloat16))
        total = total + dot(jnp.concatenate(split, axis=0), lane_hit, nt_dims)
    put = total[0:48] + total[48:96] + total[96:144]
    taken = total[144:152] > 0.5
    slot_ids = lax.broadcasted_iota(jnp.int32, (8, 128), 0) * 128 + lax.broadcasted_iota(
        jnp.int32, (8, 128), 1
    )
    live = slot_ids < count_ref[0]
    scales = (flat_scale, flat_scale, tall_scale)
    for c in range(3):
        place = jnp.where(taken, put[8 * c : 8 * c + 8], place_in[c])
        place_ref[c] = place
        speed_ref[c] = jnp.where(taken, put[24 + 8 * c : 32 + 8 * c], speed_in[c])
        sent_ref[c] = jnp.where(live, place * scales[c], far_away)


def put_ghosts(cells, ghost_ref, wanted):
    zbrick = lax.axis_index("gz")
    for level in range(4):
        rise = ((level - zbrick).astype(jnp.float32) - 0.5) * tall_scale
        for dx, cell in enumerate(cells):
            for dy in range(3):
                if not wanted(dx, dy):
                    continue
                brick = dx * 12 + dy * 4 + level
                ghost_ref[brick, 0] = cell[level, dy, 0] + (dx - 1.5) * flat_scale
                ghost_ref[brick, 1] = cell[level, dy, 1] + (dy - 1.5) * flat_scale
                ghost_ref[brick, 2] = cell[level, dy, 2] + rise
    ghost_ref[36] = jnp.full(ghost_ref.shape[1:], far_away, jnp.float32)


def own_places(middle):
    zbrick = lax.axis_index("gz")
    own = [middle[zbrick, 1, c] for c in range(3)]
    live = own[0] < 0.5 * far_away
    shifts = (0.5 * flat_scale, 0.5 * flat_scale, 0.5 * tall_scale)
    return [jnp.where(live, row - shift, -far_away) for row, shift in zip(own, shifts)], live


def put_columns(rows, column_ref):
    turned = jnp.concatenate(rows, axis=0).T
    for at in range(8 * len(rows)):
        column_ref[at] = jnp.broadcast_to(turned[:, at : at + 1], (128, 128))


def row_sums(block):
    first = block.astype(jnp.bfloat16)
    second = (block - first.astype(jnp.float32)).astype(jnp.bfloat16)
    split = jnp.concatenate([first, second], axis=1)
    sums = dot(split, jnp.ones((256, 128), jnp.bfloat16), nn_dims)
    on_line = lax.broadcasted_iota(jnp.int32, (128, 128), 0) == lax.broadcasted_iota(
        jnp.int32, (128, 128), 1
    )
    return jnp.sum(jnp.where(on_line, sums, 0.0), axis=0, keepdims=True)


def over_entries(plan_in, plan_ref, sem, late, prepare, body):
    copy = pltpu.make_async_copy(plan_in, plan_ref, sem)
    copy.start()
    prepare()
    copy.wait()

    def over_tile(near, carry):
        def over_group(group, carry):
            first = group * unrolled
            codes = [plan_ref[(first + i) >> 7, (first + i) & 127] for i in range(unrolled)]
            body(near, [(code >> 3, code & 7) for code in codes])
            return carry

        segment = near + 8 * late
        return lax.fori_loop(plan_ref[2, segment], plan_ref[2, segment + 1], over_group, carry)

    lax.fori_loop(0, 8, over_tile, 0)


def density_sums(plan_in, cells, column_ref, late, plan_ref, ghost_ref, sum_ref, sem):
    def prepare():
        put_ghosts(cells, ghost_ref, lambda dx, dy: (dx != 1) == late)
        sum_ref[...] = jnp.zeros_like(sum_ref)

    def add(near, ghosts):
        far = []
        for brick, tile in ghosts:
            x, y, z = (ghost_ref[brick, c, pl.ds(tile, 1), :] for c in range(3))
            rows = (2.0 * x, 2.0 * y, 2.0 * z, 0.5 - (x * x + y * y + z * z))
            far.append([jnp.broadcast_to(row, (8, 128)) for row in rows])
        for r in range(16):
            part = pl.ds(8 * r, 8)
            ax, ay, az, rest = (column_ref[8 * c + near, part, :] for c in range(4))
            total = sum_ref[near, part, :]
            for cx, cy, cz, cn in far:
                shrink = jnp.maximum((ax * cx + ay * cy) + (az * cz + (rest + cn)), 0.0)
                total = total + shrink * shrink * shrink
            sum_ref[near, part, :] = total

    over_entries(plan_in, plan_ref, sem, late, prepare, add)


def early_density_kernel(
    plan_in, middle, column_ref, early_ref, plan_ref, ghost_ref, sum_ref, sem
):
    own, _ = own_places(middle)
    rest = 0.5 - (own[0] * own[0] + own[1] * own[1] + own[2] * own[2])
    put_columns(own + [rest], column_ref)
    cells = (None, middle, None)
    density_sums(plan_in, cells, column_ref, False, plan_ref, ghost_ref, sum_ref, sem)
    for t in range(8):
        early_ref[t : t + 1, :] = row_sums(sum_ref[t])


def late_density_kernel(
    plan_in,
    selves_ref,
    early_ref,
    column_ref,
    behind,
    middle,
    ahead,
    slope_ref,
    plan_ref,
    ghost_ref,
    sum_ref,
    row_ref,
    sem,
):
    cells = (behind, middle, ahead)
    density_sums(plan_in, cells, column_ref, True, plan_ref, ghost_ref, sum_ref, sem)
    for t in range(8):
        row_ref[t : t + 1, :] = row_sums(sum_ref[t])
    _, live = own_places(middle)
    itself = jnp.where(live, selves_ref[...], 0.0)
    density = (row_ref[...] + early_ref[...] - itself) * density_scale
    slope_ref[...] = (-0.5 * slope_factor / cube_factor) / jnp.sqrt(1.0 + density)


def force_sums(
    plan_in, cells, slope_cells, column_ref, slopes_ref, late, plan_ref, ghost_ref, sum_ref, sem
):
    def prepare():
        put_ghosts(cells, ghost_ref, lambda dx, dy: (dy != 1) == late)
        for dy, cell in enumerate(slope_cells):
            if (dy != 1) == late:
                for dx in range(3):
                    for level in range(4):
                        ghost_ref[dx * 12 + dy * 4 + level, 3] = cell[dx * 4 + level]
        sum_ref[...] = jnp.zeros_like(sum_ref)

    def add(near, ghosts):
        far = []
        for brick, tile in ghosts:
            rows = [ghost_ref[brick, c, pl.ds(tile, 1), :] for c in range(4)]
            far.append([jnp.broadcast_to(row, (8, 128)) for row in rows])
        for r in range(16):
            part = pl.ds(8 * r, 8)
            ax, ay, az = (column_ref[8 * c + near, part, :] for c in range(3))
            slope = slopes_ref[near, part, :]
            sums = [sum_ref[8 * c + near, part, :] for c in range(3)]
            for cx, cy, cz, far_slope in far:
                dx = ax - cx
                dy = ay - cy
                dz = az - cz
                shrink = jnp.maximum(1.0 - (dx * dx + dy * dy + dz * dz), 0.0)
                weight = shrink * shrink * (shrink + (slope + far_slope))
                sums = [sums[0] + weight * dx, sums[1] + weight * dy, sums[2] + weight * dz]
            for c in range(3):
                sum_ref[8 * c + near, part, :] = sums[c]

    over_entries(plan_in, plan_ref, sem, late, prepare, add)


def early_force_kernel(
    plan_in,
    c0,
    c1,
    c2,
    column_ref,
    own_slope,
    s1,
    slopes_ref,
    early_ref,
    plan_ref,
    ghost_ref,
    sum_ref,
    sem,
):
    put_columns([own_slope[...]], slopes_ref)
    force_sums(
        plan_in,
        (c0, c1, c2),
        (None, s1, None),
        column_ref,
        slopes_ref,
        False,
        plan_ref,
        ghost_ref,
        sum_ref,
        sem,
    )
    for c in range(3):
        for t in range(8):
            early_ref[c, t : t + 1, :] = row_sums(sum_ref[8 * c + t])


def late_force_kernel(
    step,
    plan_in,
    c0,
    c1,
    c2,
    column_ref,
    s0,
    s2,
    slopes_ref,
    early_ref,
    place_in,
    speed_in,
    *rest,
):
    *outs, plan_ref, ghost_ref, sum_ref, push_ref, sem = rest
    force_sums(
        plan_in,
        (c0, c1, c2),
        (s0, None, s2),
        column_ref,
        slopes_ref,
        True,
        plan_ref,
        ghost_ref,
        sum_ref,
        sem,
    )
    for c in range(3):
        for t in range(8):
            push_ref[c, t : t + 1, :] = row_sums(sum_ref[8 * c + t])
    push = [(-cutoff * cube_factor) * (push_ref[c] + early_ref[c]) for c in range(3)]
    place = [place_in[c] for c in range(3)]
    speed = [speed_in[c] + kick * push[c] for c in range(3)]
    if step is None:
        place_ref, speed_ref = outs
        for c in range(3):
            place_ref[c] = place[c]
            speed_ref[c] = speed[c]
    else:
        slots_ref, place_ref, speed_ref, *packed = outs
        drift_and_pack(place, speed, push, slots_ref.at[step], place_ref, speed_ref, packed)


def pick_kernel(plane_ref, column_ref):
    count = lax.axis_size("gx")
    xbrick = lax.axis_index("gx")
    for dx in range(3):
        at = lax.rem(xbrick + (dx - 1 + count), count)
        for level in range(4):
            column_ref[dx * 4 + level] = plane_ref[at * 4 + level]


def shaped(*extent):
    return jax.ShapeDtypeStruct(extent, jnp.float32)


def call(kernel, outs, specs, scratch=(), mega_ops=1):
    return pl.pallas_call(
        kernel,
        out_shape=outs,
        in_specs=specs,
        out_specs=[VMEM] * len(outs),
        scratch_shapes=list(scratch),
        compiler_params=pltpu.CompilerParams(vmem_limit_bytes=24 * 2**20),
        cost_estimate=pl.CostEstimate(
            flops=mega_ops * 10**6, bytes_accessed=mega_ops * 10**5, transcendentals=0
        ),
    )


def moved(values, axis, shift):
    count = lax.axis_size(axis)
    return lax.ppermute(values, axis, [((i + shift) % count, i) for i in range(count)])


def migrants(packed):
    return (
        moved(packed[1], "gx", 1),
        moved(packed[0], "gx", -1),
        moved(packed[3], "gy", 1),
        moved(packed[2], "gy", -1),
    )


def around(values, beside):
    ends, beside = lax.optimization_barrier(
        ((moved(values, "gy", -1), moved(values, "gy", 1)), beside)
    )
    rows = jnp.stack([ends[0], values, ends[1]])
    copies = jnp.broadcast_to(rows[None], (4,) + rows.shape)
    tower = lax.all_to_all(copies, "gz", 0, 0, tiled=True)
    return (moved(tower, "gx", -1), tower, moved(tower, "gx", 1)), beside


def slope_column(values):
    count = lax.axis_size("gx") * lax.axis_size("gz")
    copies = jnp.broadcast_to(values[None], (count,) + values.shape)
    plane = lax.all_to_all(copies, ("gx", "gz"), 0, 0, tiled=True)
    (column,) = call(pick_kernel, [shaped(12, 8, 128)], [VMEM])(plane)
    return column


def per_device(positions, velocities, forces, counts, pair_tiles, pair_count, mig_slots):
    live_count = counts.reshape(1)
    total = pair_count.reshape(1)
    steps = mig_slots.shape[0]
    slots = mig_slots.reshape(steps, 4, 128)
    atoms = shaped(3, 8, 128)
    block = shaped(8, 128)
    columns = shaped(32, 128, 128)
    slope_columns = shaped(8, 128, 128)
    atoms_scratch = pltpu.VMEM((3, 8, 128), jnp.float32)
    plan_shape = jax.ShapeDtypeStruct((8, 128), jnp.int32)

    def pair_scratch(comps, sums, *found):
        return (
            pltpu.SMEM((8, 128), jnp.int32),
            pltpu.VMEM((37, comps, 8, 128), jnp.float32),
            pltpu.VMEM((8 * sums, 128, 128), jnp.float32),
            *found,
            pltpu.SemaphoreType.DMA,
        )

    rows = jnp.concatenate([a.reshape(3, 8, 128) for a in (positions, velocities, forces)], axis=0)
    place, speed, slots, *packed = call(
        pack_kernel,
        [atoms, atoms, jax.ShapeDtypeStruct(slots.shape, jnp.int32)] + [block] * 4,
        [VMEM] * 2,
    )(rows, slots)
    plan_ins = total, live_count, pair_tiles.reshape(2, 128)
    plan_outs = [plan_shape, plan_shape, block]
    plans = call(plan_kernel, plan_outs, [SMEM, SMEM, VMEM])(*plan_ins)
    for n in range(steps):
        place, speed, sent = call(
            functools.partial(unpack_kernel, n), [atoms, atoms, atoms], [SMEM] + [VMEM] * 7
        )(live_count, place, speed, slots, *migrants(packed))
        cells, plans = around(sent, plans)
        density_plan, force_plan, selves = plans
        if n == 0:
            plans = call(plan_kernel, plan_outs, [SMEM, SMEM] + [VMEM] * 4)(*plan_ins, *cells)
        column, early = call(
            early_density_kernel,
            [columns, block],
            [ANY, VMEM],
            pair_scratch(3, 1),
            mega_ops=60,
        )(density_plan, cells[1])
        (slope,) = call(
            late_density_kernel,
            [block],
            [ANY] + [VMEM] * 6,
            pair_scratch(3, 1, pltpu.VMEM((8, 128), jnp.float32)),
        )(density_plan, selves, early, column, *cells)
        here = slope_column(slope)
        below, above = moved(here, "gy", -1), moved(here, "gy", 1)
        slopes, early = call(
            early_force_kernel,
            [slope_columns, atoms],
            [ANY] + [VMEM] * 6,
            pair_scratch(4, 3),
            mega_ops=60,
        )(force_plan, *cells, column, slope, here)
        last = n + 1 == steps
        place, speed, *packed = call(
            functools.partial(late_force_kernel, None if last else n + 1),
            [atoms, atoms] + [block] * (0 if last else 4),
            [ANY] + [VMEM] * (10 if last else 11),
            pair_scratch(4, 3, atoms_scratch),
        )(
            force_plan,
            *cells,
            column,
            below,
            above,
            slopes,
            early,
            place,
            speed,
            *(() if last else (slots,)),
        )
    return (place.reshape(positions.shape), speed.reshape(velocities.shape))


def solution(mesh):
    placed = (
        P(None, "gx", "gy", "gz", None),
        P(None, "gx", "gy", "gz", None),
        P(None, "gx", "gy", "gz", None),
        P("gx", "gy", "gz"),
        P(None, "gx", "gy", "gz", None),
        P("gx", "gy", "gz"),
        P(None, None, "gx", "gy", "gz", None),
    )
    return jax.shard_map(
        per_device,
        mesh=mesh,
        in_specs=placed,
        out_specs=(P(None, "gx", "gy", "gz", None), P(None, "gx", "gy", "gz", None)),
        check_vma=False,
    )
```
